512 devices in a mesh: gx: 16 (over z, x_hi), gy: 16 (over y, core), band: 2 (over x_lo).
Axes of the slice: x: 4 (x_hi: 2, x_lo: 2; x = x_hi * 2 + x_lo), y: 8, z: 8, core: 2. Of those that a mesh axis runs over, the one named last changes fastest.
Arguments:
- orbitals: float32 [2, 4, 256, 256, 128], P(None, 'band', 'gx', 'gy'), may hold values from -6 to 6
- potential: float32 [256, 256, 128], P('gx', 'gy'), may hold values from -2 to 2
- corners: int32 [1024, 3], P(('gx', 'gy')), may hold values from 0 to 255, as said below
- counts: int32 [1024], P(('gx', 'gy')), may hold values from 1 to 4, as said below
- coupling: float32 [1024, 4, 4], P(('gx', 'gy')), may hold values from -7.5 to 7.5
- projectors: float32 [4, 4096], replicated
- occupations: float32 [4], P('band'), may hold values from 0.05 to 0.4
Outputs:
- propagated: float32 [2, 4, 256, 256, 128], P(None, 'band', 'gx', 'gy')
- density: float32 [256, 256, 128], P('gx', 'gy')
The draws below stay inside these ranges and needn't reach their ends.
Inputs may be any that keep to these rules, and one draw needn't show every extreme that they name: An atom held by the pencil at index i of gx and j of gy has corners[a,0] in [i * 16, (i + 1) * 16) and corners[a,1] in [j * 16, (j + 1) * 16); every pencil holds an atom with x offset 16 - 1 in its pencil and one with y offset 16 - 1. `counts`: every pencil's atoms take each count from 1 to 4.
All inputs are finite; a program needn't handle non-finite values.
Results may differ from the reference program's by a relative error of at most 0.0001.
Values sent between devices are 32-bit elements; how exact they have to be, the bound alone decides.
A program may use at most 128 MiB of HBM per device.

```python
import math
import jax
import jax.numpy as jnp
from jax import lax

CX = 16
CY = 16
NZ = 128
ATOM_DEV = 4
BOX = 16
NPROJ = 4
ORBITALS = 4
NX = 256
NY = 256
ATOMS = 1024


def pencil_rank(key):
    pencils = NX // CX * (NY // CY)
    scores = jax.random.randint(key, (pencils, ATOM_DEV), 0, 1 << 20) * ATOM_DEV
    scores = scores + jnp.arange(ATOM_DEV, dtype=jnp.int32)[None, :]
    ordering = jnp.argsort(scores, axis=1, stable=True)
    return jnp.argsort(ordering, axis=1, stable=True).reshape(-1).astype(jnp.int32)


def draw_corners(key, part):
    key = jax.random.fold_in(key, 11)
    subkeys = jax.random.split(key, 5)
    atom_total = ATOM_DEV * (NX // CX) * (NY // CY)
    owner_index = jnp.arange(atom_total, dtype=jnp.int32) // ATOM_DEV
    pencil_x = owner_index // (NY // CY)
    pencil_y = owner_index % (NY // CY)
    rank_x = pencil_rank(subkeys[0])
    rank_y = pencil_rank(subkeys[1])
    offset_x = jnp.where(rank_x == 0, CX - 1, jax.random.randint(subkeys[2], (atom_total,), 0, CX))
    offset_y = jnp.where(rank_y == 0, CY - 1, jax.random.randint(subkeys[3], (atom_total,), 0, CY))
    offset_z = jax.random.randint(subkeys[4], (atom_total,), 0, NZ)
    offset_z = offset_z.at[0].set(NZ - 1)
    return jnp.stack([pencil_x * CX + offset_x, pencil_y * CY + offset_y, offset_z], axis=1).astype(jnp.int32)


def draw_counts(key, part):
    key = jax.random.fold_in(key, 12)
    return (1 + pencil_rank(key) % NPROJ).astype(jnp.int32)


def draw_projectors(key, part):
    key = jax.random.fold_in(key, 13)
    cell_index = jnp.arange(BOX * BOX * BOX, dtype=jnp.int32)
    middle = (BOX - 1) / 2.0
    along_x = (cell_index // (BOX * BOX)).astype(jnp.float32) - middle
    along_y = (cell_index // BOX % BOX).astype(jnp.float32) - middle
    along_z = (cell_index % BOX).astype(jnp.float32) - middle
    spread = BOX / 6.0
    envelope = jnp.exp(-(along_x * along_x + along_y * along_y + along_z * along_z) / (2.0 * spread * spread))
    amplitude = (math.pi * spread * spread) ** (-0.75)
    random_part = jnp.clip(jax.random.normal(key, (NPROJ, BOX * BOX * BOX), jnp.float32), -4.0, 4.0)
    return (amplitude * envelope[None, :] * random_part).astype(jnp.float32)


def shard_levels(key, extent, shards, least, high):
    def one(axis_at, parts):
        steps = jax.random.uniform(jax.random.fold_in(jax.random.fold_in(key, 6), axis_at), (parts,), jnp.float32, least / len(shards), high / len(shards))
        return jnp.repeat(jnp.exp(steps), extent[axis_at] // parts).reshape((-1,) + (1,) * (len(extent) - axis_at - 1))

    factor_of = one(*shards[0])
    for cut in shards[1:]:
        factor_of = factor_of * one(*cut)
    return factor_of


def centred(stream_key, extent, scale, reach, shards=(), kind=jnp.bfloat16):
    gain = shard_levels(stream_key, extent, shards, -0.22, 0.18) if shards else 1.0
    entries = jax.random.normal(stream_key, extent, jnp.float32) * scale * gain
    return jnp.minimum(jnp.maximum(entries, -reach), reach).astype(kind)


def setup_inputs(seed: int = 0) -> dict:
    arg_keys = jax.random.split(jax.random.key(seed), 8)
    orbitals = centred(arg_keys[0], (2, ORBITALS, NX, NY, NZ), 1.0, 6.0, ((1, 2), (2, 16), (3, 16)), jnp.float32)
    potential = jnp.clip(jax.random.uniform(arg_keys[1], (NX, NY, NZ), jnp.float32, -2.0, 2.0) * shard_levels(arg_keys[1], (NX, NY, NZ), ((0, 16), (1, 16)), -0.4, 0.0), -2.0, 2.0)
    corners = draw_corners(jax.random.fold_in(arg_keys[7], 71), 0)
    counts = draw_counts(jax.random.fold_in(arg_keys[7], 71), 0)
    coupling = centred(arg_keys[4], (ATOMS, NPROJ, NPROJ), 2.5, 7.5, ((0, 256),), jnp.float32)
    projectors = draw_projectors(jax.random.fold_in(arg_keys[7], 71), 0)
    occupations = jnp.clip(jnp.exp(math.log(0.4) - 2.0794415 * jax.random.uniform(arg_keys[6], (ORBITALS,), jnp.float32) ** shard_levels(arg_keys[6], (ORBITALS,), ((0, 2),), -0.2, 0.2)), 0.05, 0.4)
    return {"orbitals": orbitals, "potential": potential, "corners": corners, "counts": counts, "coupling": coupling, "projectors": projectors, "occupations": occupations}


time_step = 0.12
center_weight = -2.5
near_weight = 4.0 / 3.0
far_weight = -1.0 / 12.0
highest = lax.Precision.HIGHEST


def laplace(fields):
    near = (jnp.roll(fields, -1, 0) + jnp.roll(fields, 1, 0)
            + jnp.roll(fields, -1, 1) + jnp.roll(fields, 1, 1)
            + jnp.roll(fields, -1, 2) + jnp.roll(fields, 1, 2))
    far = (jnp.roll(fields, -2, 0) + jnp.roll(fields, 2, 0)
           + jnp.roll(fields, -2, 1) + jnp.roll(fields, 2, 1)
           + jnp.roll(fields, -2, 2) + jnp.roll(fields, 2, 2))
    return 3.0 * center_weight * fields + near_weight * near + far_weight * far


def apply_field(fields, potential, index_x, index_y, index_z, projectors, coupled):
    atom_total = index_x.shape[0]
    place_x = index_x[:, :, None, None]
    place_y = index_y[:, None, :, None]
    place_z = index_z[:, None, None, :]
    boxes = fields[place_x, place_y, place_z]
    intersection = jnp.dot(boxes.reshape(atom_total, -1), projectors.T, precision=highest,
                      preferred_element_type=jnp.float32)
    coefficients = jnp.einsum("aji,ai->aj", coupled, intersection, precision=highest,
                              preferred_element_type=jnp.float32)
    values = jnp.dot(coefficients, projectors, precision=highest,
                     preferred_element_type=jnp.float32).reshape(boxes.shape)
    projected = jnp.zeros_like(fields).at[place_x, place_y, place_z].add(values)
    return -0.5 * laplace(fields) + potential * fields + projected


def reference(orbitals, potential, corners, counts, coupling, projectors, occupations):
    steps_box = jnp.arange(BOX, dtype=jnp.int32)
    index_x = ((corners[:, 0:1] + steps_box[None, :]) % NX).astype(jnp.int32)
    index_y = ((corners[:, 1:2] + steps_box[None, :]) % NY).astype(jnp.int32)
    index_z = ((corners[:, 2:3] + steps_box[None, :]) % NZ).astype(jnp.int32)
    symmetric = 0.5 * (coupling + jnp.swapaxes(coupling, 1, 2))
    active = (jnp.arange(NPROJ, dtype=jnp.int32)[None, :] < counts[:, None]).astype(jnp.float32)
    coupled = symmetric * active[:, :, None] * active[:, None, :]

    def apply_stack(stack):
        flat = stack.reshape((-1, NX, NY, NZ))
        result = lax.map(lambda single: apply_field(single, potential, index_x, index_y, index_z,
                                                    projectors, coupled), flat)
        return result.reshape(stack.shape)

    series = orbitals
    taylor_term = orbitals
    for power in range(1, 5):
        applied = apply_stack(taylor_term)
        factor = time_step / power
        taylor_term = jnp.stack([factor * applied[1], -factor * applied[0]])
        series = series + taylor_term
    density = jnp.sum(occupations[:, None, None, None] * (series[0] * series[0] + series[1] * series[1]), axis=0)
    return series, density
```

```python
import jax
import jax.numpy as jnp
from jax import lax
from jax.experimental import pallas as pl
from jax.experimental.pallas import tpu as pltpu
from jax.sharding import PartitionSpec as P

BOX = 16
NPROJ = 4
CELL = 16
LANES = 128
FIELDS = 4
STEPS = 4
TIME_STEP = 0.12
MESH = pl.DeviceIdType.MESH
f32 = jnp.float32
bf16 = jnp.bfloat16

NEAR = tuple((dx, dy) for dx in (-1, 1, 0) for dy in (-1, 1, 0) if (dx, dy) != (0, 0))
ABOVE = ((1, 1), (1, 0), (0, 1))
SIDES = ((1, 0), (-1, 0), (0, 1), (0, -1))


def peer(step_x, step_y):
    size_x, size_y = lax.axis_size("gx"), lax.axis_size("gy")
    return (
        lax.rem(lax.axis_index("gx") + step_x + size_x, size_x),
        lax.rem(lax.axis_index("gy") + step_y + size_y, size_y),
        lax.axis_index("band"),
    )


def partner():
    return (lax.axis_index("gx"), lax.axis_index("gy"), 1 - lax.axis_index("band"))


def lane_index(shape):
    return lax.broadcasted_iota(jnp.int32, shape, len(shape) - 1)


def row_index(shape):
    return lax.broadcasted_iota(jnp.int32, shape, len(shape) - 2)


def halves(x):
    high = x.astype(bf16)
    low = (x - high.astype(f32)).astype(bf16)
    return high, low


def thirds(x):
    high = x.astype(bf16)
    rest = x - high.astype(f32)
    mid = rest.astype(bf16)
    low = (rest - mid.astype(f32)).astype(bf16)
    return high, mid, low


def dot_exact(x, pick):
    rows = x.shape[0]
    r = jnp.dot(jnp.concatenate(thirds(x), axis=0), pick, preferred_element_type=f32)
    return r[:rows] + r[rows : 2 * rows] + r[2 * rows :]


def kernel(
    fields_ref, potential_ref, info_ref, projectors_ref, occupations_ref,
    propagated_ref, density_ref,
    term, side_y, local_part, series, pot, info_in, boxes, placed_y, frames,
    pick_in, pick_out, compact, expand, coupled, coef, split_term, slabs, split_values,
    shares, shares_out, shares_in, dens, dens_in, result,
    load_sem, info_send, info_recv, side_send, side_recv, share_send, share_recv,
    dens_send, dens_recv, store_sem,
):
    inner = pl.ds(2, CELL)

    barrier = pltpu.get_barrier_semaphore()
    for d in NEAR:
        pl.semaphore_signal(barrier, inc=1, device_id=peer(*d), device_id_type=MESH)
    pl.semaphore_signal(barrier, inc=1, device_id=partner(), device_id_type=MESH)

    load_fields = [
        pltpu.make_async_copy(fields_ref.at[f], term.at[0, f, inner], load_sem.at[f])
        for f in range(FIELDS)
    ]
    load_potential = pltpu.make_async_copy(potential_ref, pot, load_sem.at[FIELDS])
    for copy in load_fields:
        copy.start()
    load_potential.start()

    r = row_index((2 * LANES, LANES))
    l = lane_index((2 * LANES, LANES))
    compact[...] = jnp.where((l < 64) & (l % 16 == r // 16), 1.0, 0.0).astype(bf16)
    r = row_index((LANES, 2 * LANES))
    l = lane_index((LANES, 2 * LANES))
    expand[...] = jnp.where(r % 16 == l // 16, 1.0, 0.0).astype(bf16)
    fold = jnp.where(
        row_index((LANES, LANES)) % 16 == lane_index((LANES, LANES)) % 16, 1.0, 0.0
    ).astype(bf16)

    own_group = row_index((8, LANES)) == lane_index((8, LANES)) // 16
    for j in range(NPROJ):
        pieces = []
        for c in range(2 * BOX):
            line = projectors_ref[j : j + 1, c * LANES : (c + 1) * LANES]
            pieces.append(jnp.where(own_group, jnp.broadcast_to(line, (8, LANES)), 0.0))
        boxes[j] = dot_exact(jnp.concatenate(pieces, axis=0), fold).reshape(BOX, BOX, LANES)

    pl.semaphore_wait(barrier, len(NEAR) + 1)

    info_copies = [
        pltpu.make_async_remote_copy(
            src_ref=info_ref, dst_ref=info_in.at[i], send_sem=info_send.at[i],
            recv_sem=info_recv.at[i], device_id=peer(*d), device_id_type=MESH,
        )
        for i, d in enumerate(ABOVE)
    ]
    for copy in info_copies:
        copy.start()

    def side_copies(n):
        copies = []
        for k, d in enumerate(SIDES):
            if k == 0:
                src, dst = term.at[n, :, pl.ds(CELL, 2)], term.at[n, :, pl.ds(0, 2)]
            elif k == 1:
                src, dst = term.at[n, :, pl.ds(2, 2)], term.at[n, :, pl.ds(CELL + 2, 2)]
            else:
                rows = pl.ds(CELL - 2, 2) if k == 2 else pl.ds(0, 2)
                src, dst = term.at[n, :, inner, rows], side_y.at[n, :, :, rows]
            copies.append(
                pltpu.make_async_remote_copy(
                    src_ref=src, dst_ref=dst, send_sem=side_send.at[n, k],
                    recv_sem=side_recv.at[n, k], device_id=peer(*d), device_id_type=MESH,
                )
            )
        return copies

    def share_copies(n):
        return [
            pltpu.make_async_remote_copy(
                src_ref=shares_out.at[n, k], dst_ref=shares_in.at[n, k],
                send_sem=share_send.at[n, k], recv_sem=share_recv.at[n, k],
                device_id=peer(*d), device_id_type=MESH,
            )
            for k, d in enumerate(NEAR)
        ]

    for copy in load_fields:
        copy.wait()
    for copy in side_copies(0):
        copy.start()

    def split_first(x, _):
        for f in range(FIELDS):
            high, low = halves(term[0, f, x + 2])
            split_term[f, x, :, :LANES] = high
            split_term[f, x, :, LANES:] = low
        return 0

    lax.fori_loop(0, CELL, split_first, 0)
    load_potential.wait()

    for copy in info_copies:
        copy.wait_recv()

    lane = lane_index((1, LANES))
    upper = lane >= 64
    from_xy, from_x, from_y = (info_in.at[i] for i in range(3))
    near_x = []
    for h in range(2):
        a, b = (info_ref, from_x) if h == 0 else (from_y, from_xy)
        near_x.append(jnp.where(upper, b[...], a[...]))
    for h in range(2):
        depth = (near_x[h][2:3].astype(jnp.int32) + lane % 16) % LANES
        hit = row_index((LANES, LANES)) == depth
        pick = jnp.where(hit, 1.0, 0.0).astype(bf16)
        pick_in[:LANES, h * LANES : (h + 1) * LANES] = pick
        pick_in[LANES:, h * LANES : (h + 1) * LANES] = pick
        pick_out[:, h * LANES : (h + 1) * LANES] = pick
        pick_out[:, (h + 2) * LANES : (h + 3) * LANES] = pick
        for i in range(NPROJ):
            rows = near_x[h][8 + 4 * i : 12 + 4 * i]
            coupled[i, :, h * LANES : (h + 1) * LANES] = jnp.concatenate([rows] * FIELDS, axis=0)

    row = row_index((CELL, LANES))
    for h in range(2):
        at_y = near_x[h][1:2].astype(jnp.int32)
        shift = jnp.broadcast_to(at_y if h == 0 else CELL - at_y, (CELL, LANES))
        bits = []
        for b in range(4):
            step = 1 << b
            stays = row >= step if h == 0 else row < CELL - step
            moved = (shift // step) % 2 == 1
            bits.append((step if h == 0 else CELL - step, moved & stays, moved & ~stays))
        whole = shift >= CELL

        def place_y(i, _, bits=bits, whole=whole, h=h):
            for j in range(NPROJ):
                v = boxes[j, i]
                for step, keep, drop in bits:
                    rolled = pltpu.roll(v, step, 0)
                    v = jnp.where(keep, rolled, jnp.where(drop, 0.0, v))
                placed_y[h, j, i] = jnp.where(whole, 0.0, v)
            return 0

        lax.fori_loop(0, BOX, place_y, 0)

    for h in range(2):
        at_x = jnp.broadcast_to(near_x[h][0:1].astype(jnp.int32), (CELL, LANES))
        above = jnp.broadcast_to(upper, (CELL, LANES))
        down = [~above & ((at_x // (1 << b)) % 2 == 1) for b in range(4)]
        up = [above & (((CELL - at_x) // (1 << b)) % 2 == 1) for b in range(4)]
        whole = above & (at_x == 0)

        def place_x(j, _, down=down, up=up, whole=whole, h=h):
            v = [placed_y[h, j, i] for i in range(BOX)]
            zero = jnp.zeros((CELL, LANES), f32)
            for b in range(4):
                step = 1 << b
                v = [
                    jnp.where(
                        down[b],
                        v[x - step] if x >= step else zero,
                        jnp.where(up[b], v[x + step] if x + step < CELL else zero, v[x]),
                    )
                    for x in range(CELL)
                ]
            for x in range(CELL):
                frames[h, j, x] = jnp.where(whole, 0.0, v[x])
            return 0

        lax.fori_loop(0, NPROJ, place_x, 0)

    def send_shares(n):
        def slab(f, _):
            cells = split_term[f].reshape(CELL * CELL, 2 * LANES)
            slabs[f] = jnp.dot(cells, pick_in[...], preferred_element_type=f32).reshape(
                CELL, CELL, 2 * LANES
            )
            return 0

        lax.fori_loop(0, FIELDS, slab, 0)
        sums = []
        for h in range(2):

            def add(x, totals, h=h):
                frame = [frames[h, j, x] for j in range(NPROJ)]
                new = []
                for f in range(FIELDS):
                    part = slabs[f, x, :, h * LANES : (h + 1) * LANES]
                    for j in range(NPROJ):
                        product = part * frame[j]
                        new.append(totals[f * NPROJ + j] + product[:8] + product[8:])
                return tuple(new)

            zero = jnp.zeros((8, LANES), f32)
            totals = lax.fori_loop(0, CELL, add, (zero,) * (FIELDS * NPROJ))
            sums.append(jnp.concatenate([jnp.sum(t, axis=0, keepdims=True) for t in totals], axis=0))
        lines = dot_exact(jnp.concatenate(sums, axis=1), compact[...])
        mine = jnp.zeros((NPROJ, LANES), f32)
        lane4 = lane_index((NPROJ, LANES))
        for f in range(FIELDS):
            mine = mine + jnp.where(lane4 // 16 == f, lines[4 * f : 4 * f + 4], 0.0)
        shares[...] = mine
        slot = (lane4 // 4) % 4
        valid = lane4 < 64
        for k, (dx, dy) in enumerate(NEAR):
            keep = valid
            if dx:
                keep = keep & (slot % 2 == (1 if dx == 1 else 0))
            if dy:
                keep = keep & (slot // 2 == (1 if dy == 1 else 0))
            moved = pltpu.roll(mine, (4 * dx + 8 * dy) % LANES, 1)
            shares_out[n, k] = jnp.where(keep, moved, 0.0)
        for copy in share_copies(n):
            copy.start()

    send_shares(0)

    row16 = row_index((CELL, LANES))

    def make_term(n, store):
        last = n - 1
        for copy in side_copies(last):
            copy.wait_recv()

        def stencil(x, _):
            v = pot[x]
            for f in range(FIELDS):
                u = term[last, f, x + 2]
                edge = side_y[last, f, x]
                near = term[last, f, x + 1] + term[last, f, x + 3]
                far = term[last, f, x] + term[last, f, x + 4]
                near = near + pltpu.roll(jnp.where(row16 == 0, edge, u), CELL - 1, 0)
                near = near + pltpu.roll(jnp.where(row16 == CELL - 1, edge, u), 1, 0)
                far = far + pltpu.roll(jnp.where(row16 < 2, edge, u), CELL - 2, 0)
                far = far + pltpu.roll(jnp.where(row16 >= CELL - 2, edge, u), 2, 0)
                near = near + pltpu.roll(u, 1, 1) + pltpu.roll(u, LANES - 1, 1)
                far = far + pltpu.roll(u, 2, 1) + pltpu.roll(u, LANES - 2, 1)
                local_part[f, x] = (v + 3.75) * u + (-2.0 / 3.0) * near + (1.0 / 24.0) * far
            return 0

        lax.fori_loop(0, CELL, stencil, 0)

        for copy in share_copies(last):
            copy.wait_recv()
        total = shares[...]
        for k in range(len(NEAR)):
            total = total + shares_in[last, k]
        field_of_row = row_index((FIELDS * NPROJ, LANES)) // NPROJ
        field_of_lane = lane_index((FIELDS * NPROJ, LANES)) // 16
        lines = [
            jnp.where(
                field_of_row == field_of_lane,
                jnp.broadcast_to(total[i : i + 1], (FIELDS * NPROJ, LANES)),
                0.0,
            )
            for i in range(NPROJ)
        ]
        wide = dot_exact(jnp.concatenate(lines, axis=0), expand[...])
        rows = FIELDS * NPROJ
        weights = coupled[0] * wide[:rows]
        for i in range(1, NPROJ):
            weights = weights + coupled[i] * wide[i * rows : (i + 1) * rows]
        coef[...] = weights

        for h in range(2):
            lanes = pl.ds(h * LANES, LANES)

            def spread(x, _, h=h, lanes=lanes):
                frame = [frames[h, j, x] for j in range(NPROJ)]
                for f in range(FIELDS):
                    value = coef[f * NPROJ : f * NPROJ + 1, lanes] * frame[0]
                    for j in range(1, NPROJ):
                        value = value + coef[f * NPROJ + j : f * NPROJ + j + 1, lanes] * frame[j]
                    high, low = halves(value)
                    split_values[f, x, :, h * LANES : (h + 1) * LANES] = high
                    split_values[f, x, :, (h + 2) * LANES : (h + 3) * LANES] = low
                return 0

            lax.fori_loop(0, CELL, spread, 0)

        factor = TIME_STEP / (jnp.zeros((CELL, LANES), f32) + n)
        for f in range(FIELDS):
            source = (f + 2) % 4
            projected = lax.dot_general(
                split_values[source].reshape(CELL * CELL, 4 * LANES), pick_out[...],
                (((1,), (1,)), ((), ())), preferred_element_type=f32,
            )
            signed = factor if f < 2 else -factor
            local_part[source] = local_part[source] + projected.reshape(CELL, CELL, LANES)
            store(f, source, signed)

    def step(n, _):
        def store(f, source, signed):
            def line(x, _):
                value = signed * local_part[source, x]
                term[n, f, x + 2] = value
                high, low = halves(value)
                split_term[f, x, :, :LANES] = high
                split_term[f, x, :, LANES:] = low
                return 0

            lax.fori_loop(0, CELL, line, 0)

        make_term(n, store)
        for copy in side_copies(n):
            copy.start()
        send_shares(n)
        return 0

    lax.fori_loop(1, STEPS, step, 0)

    def store_last(f, source, signed):
        def line(x, _):
            total = term[0, f, x + 2] + term[1, f, x + 2]
            total = total + term[2, f, x + 2] + term[3, f, x + 2]
            result[f, x] = total + signed * local_part[source, x]
            return 0

        lax.fori_loop(0, CELL, line, 0)

    make_term(STEPS, store_last)

    def density(x, _):
        total = jnp.zeros((CELL, LANES), f32)
        for f in range(FIELDS):
            total = total + occupations_ref[f % 2 : f % 2 + 1, :] * (result[f, x] * result[f, x])
        dens[x] = total
        return 0

    lax.fori_loop(0, CELL, density, 0)
    send = pltpu.make_async_remote_copy(
        src_ref=dens, dst_ref=dens_in, send_sem=dens_send, recv_sem=dens_recv,
        device_id=partner(), device_id_type=MESH,
    )
    send.start()
    store_result = pltpu.make_async_copy(result, propagated_ref, store_sem)
    store_result.start()
    for copy in info_copies:
        copy.wait_send()

    def drain(n, _):
        for copy in side_copies(n) + share_copies(n):
            copy.wait_send()
        return 0

    lax.fori_loop(0, STEPS, drain, 0)
    send.wait_recv()

    density_ref[...] = dens[...] + dens_in[...]
    send.wait_send()
    store_result.wait()


def atom_lines(corners, counts, coupling):
    symmetric = 0.5 * (coupling + jnp.swapaxes(coupling, 1, 2))
    active = (jnp.arange(NPROJ, dtype=jnp.int32)[None, :] < counts[:, None]).astype(f32)
    coupled = symmetric * active[:, :, None] * active[:, None, :]
    corner = jnp.concatenate([corners[:, :2] % CELL, corners[:, 2:]], axis=1).astype(f32)
    columns = jnp.swapaxes(coupled, 1, 2).reshape(-1, NPROJ * NPROJ)
    rows = jnp.concatenate([corner, jnp.zeros((corner.shape[0], 5), f32), columns], axis=1)
    return jnp.tile(jnp.repeat(rows.T, BOX, axis=1), (1, 2))


def local(orbitals, potential, corners, counts, coupling, projectors, occupations):
    fields = orbitals.reshape(FIELDS, CELL, CELL, LANES)
    info = atom_lines(corners, counts, coupling)
    weights = jnp.broadcast_to(occupations[:, None], (2, LANES))
    vmem = pl.BlockSpec(memory_space=pltpu.VMEM)
    hbm = pl.BlockSpec(memory_space=pl.ANY)
    grid = (CELL, CELL, LANES)
    dma = pltpu.SemaphoreType.DMA
    propagated, density = pl.pallas_call(
        kernel,
        out_shape=(
            jax.ShapeDtypeStruct((FIELDS,) + grid, f32),
            jax.ShapeDtypeStruct(grid, f32),
        ),
        in_specs=[hbm, hbm, vmem, vmem, vmem],
        out_specs=(hbm, vmem),
        scratch_shapes=[
            pltpu.VMEM((STEPS, FIELDS, CELL + 4, CELL, LANES), f32),
            pltpu.VMEM((STEPS, FIELDS) + grid, f32),
            pltpu.VMEM((FIELDS,) + grid, f32),
            pltpu.VMEM((8, LANES), f32),
            pltpu.VMEM(grid, f32),
            pltpu.VMEM((3, 24, LANES), f32),
            pltpu.VMEM((NPROJ,) + grid, f32),
            pltpu.VMEM((2, NPROJ) + grid, f32),
            pltpu.VMEM((2, NPROJ) + grid, f32),
            pltpu.VMEM((2 * LANES, 2 * LANES), bf16),
            pltpu.VMEM((LANES, 4 * LANES), bf16),
            pltpu.VMEM((2 * LANES, LANES), bf16),
            pltpu.VMEM((LANES, 2 * LANES), bf16),
            pltpu.VMEM((NPROJ, FIELDS * NPROJ, 2 * LANES), f32),
            pltpu.VMEM((FIELDS * NPROJ, 2 * LANES), f32),
            pltpu.VMEM((FIELDS, CELL, CELL, 2 * LANES), bf16),
            pltpu.VMEM((FIELDS, CELL, CELL, 2 * LANES), f32),
            pltpu.VMEM((FIELDS, CELL, CELL, 4 * LANES), bf16),
            pltpu.VMEM((NPROJ, LANES), f32),
            pltpu.VMEM((STEPS, len(NEAR), NPROJ, LANES), f32),
            pltpu.VMEM((STEPS, len(NEAR), NPROJ, LANES), f32),
            pltpu.VMEM(grid, f32),
            pltpu.VMEM(grid, f32),
            pltpu.VMEM((FIELDS,) + grid, f32),
            dma((FIELDS + 1,)),
            dma((3,)),
            dma((3,)),
            dma((STEPS, 4)),
            dma((STEPS, 4)),
            dma((STEPS, len(NEAR))),
            dma((STEPS, len(NEAR))),
            dma,
            dma,
            dma,
        ],
        compiler_params=pltpu.CompilerParams(
            collective_id=1, has_side_effects=True, vmem_limit_bytes=48 * 2**20
        ),
    )(fields, potential, info, projectors, weights)
    return propagated.reshape(orbitals.shape), density


def solution(mesh):
    placed = (
        P(None, "band", "gx", "gy", None),
        P("gx", "gy", None),
        P(("gx", "gy"), None),
        P(("gx", "gy")),
        P(("gx", "gy"), None, None),
        P(),
        P("band"),
    )
    return jax.shard_map(
        local,
        mesh=mesh,
        in_specs=placed,
        out_specs=(P(None, "band", "gx", "gy", None), P("gx", "gy", None)),
        check_vma=False,
    )
```

```python
import jax
import jax.numpy as jnp
from jax import lax
from jax.experimental import pallas as pl
from jax.experimental.pallas import tpu as pltpu
from jax.sharding import PartitionSpec as P

BOX = 16
NPROJ = 4
CELL = 16
LANES = 128
FIELDS = 4
STEPS = 4
PAIR = 2
UNROLL = 4
VMEM_BYTES = 60 * 2**20
TIME_STEP = 0.12
MESH = pl.DeviceIdType.MESH
f32 = jnp.float32
bf16 = jnp.bfloat16

NEAR = tuple((dx, dy) for dx in (-1, 1, 0) for dy in (-1, 1, 0) if (dx, dy) != (0, 0))
ABOVE = ((1, 1), (1, 0), (0, 1))
SIDES = ((1, 0), (-1, 0), (0, 1), (0, -1))


def peer(step_x, step_y):
    size_x, size_y = lax.axis_size("gx"), lax.axis_size("gy")
    return (
        lax.rem(lax.axis_index("gx") + step_x + size_x, size_x),
        lax.rem(lax.axis_index("gy") + step_y + size_y, size_y),
        lax.axis_index("band"),
    )


def partner():
    return (lax.axis_index("gx"), lax.axis_index("gy"), 1 - lax.axis_index("band"))


def lane_index(shape):
    return lax.broadcasted_iota(jnp.int32, shape, len(shape) - 1)


def row_index(shape):
    return lax.broadcasted_iota(jnp.int32, shape, len(shape) - 2)


def halves(x):
    high = x.astype(bf16)
    low = (x - high.astype(f32)).astype(bf16)
    return high, low


def thirds(x):
    high = x.astype(bf16)
    rest = x - high.astype(f32)
    mid = rest.astype(bf16)
    low = (rest - mid.astype(f32)).astype(bf16)
    return high, mid, low


def dot_exact(x, pick):
    rows = x.shape[0]
    r = jnp.dot(jnp.concatenate(thirds(x), axis=0), pick, preferred_element_type=f32)
    return r[:rows] + r[rows : 2 * rows] + r[2 * rows :]


def kernel(
    fields_ref, potential_ref, corners_hbm, counts_hbm, coupling_hbm, projectors_ref, occupations_hbm,
    propagated_ref, density_ref,
    term, side_y, local_part, pot, table, corners_ref, counts_ref, coupling_ref, occupations_ref, info, info_in, boxes, placed_y, frames,
    pick_in, pick_out, compact, expand, coupled, coef, split_term, slabs, split_values, projected,
    shares, shares_out, shares_in, dens, dens_in,
    load_sem, info_send, info_recv, side_send, side_recv, share_send, share_recv,
    dens_send, dens_recv,
):
    inner = pl.ds(2, CELL)

    barrier = pltpu.get_barrier_semaphore()
    for d in NEAR:
        pl.semaphore_signal(barrier, inc=1, device_id=peer(*d), device_id_type=MESH)
    pl.semaphore_signal(barrier, inc=1, device_id=partner(), device_id_type=MESH)

    load_fields = [
        pltpu.make_async_copy(fields_ref.at[f], term.at[0, f, inner], load_sem.at[f])
        for f in range(FIELDS)
    ]
    load_potential = pltpu.make_async_copy(potential_ref, pot, load_sem.at[FIELDS])
    load_table = pltpu.make_async_copy(projectors_ref, table, load_sem.at[FIELDS + 1])
    load_atoms = [
        pltpu.make_async_copy(src, dst, load_sem.at[FIELDS + 2 + i])
        for i, (src, dst) in enumerate(
            (
                (corners_hbm, corners_ref),
                (counts_hbm, counts_ref),
                (coupling_hbm, coupling_ref),
                (occupations_hbm, occupations_ref),
            )
        )
    ]
    for copy in load_atoms:
        copy.start()
    load_table.start()
    for copy in load_fields:
        copy.start()
    load_potential.start()

    lane = lane_index((1, LANES))
    atom_of_lane = (lane // BOX) % 4

    for copy in load_atoms:
        copy.wait()

    def over_atoms(values):
        values = [jnp.broadcast_to(v, (1, LANES)) for v in values]
        line = jnp.where(atom_of_lane == 0, values[0], values[1])
        line = jnp.where(atom_of_lane == 2, values[2], line)
        return jnp.where(atom_of_lane == 3, values[3], line)

    for axis in range(3):
        line = over_atoms([corners_ref[a : a + 1, axis : axis + 1] for a in range(4)])
        line = line % CELL if axis < 2 else line
        info[axis : axis + 1] = line.astype(f32)
    count = over_atoms([counts_ref[0:1, a : a + 1] for a in range(4)])
    entry = [
        [over_atoms([coupling_ref[a, j : j + 1, i : i + 1] for a in range(4)]) for i in range(NPROJ)]
        for j in range(NPROJ)
    ]
    for i in range(NPROJ):
        for j in range(NPROJ):
            line = jnp.where(count > max(i, j), 0.5 * (entry[j][i] + entry[i][j]), 0.0)
            info[8 + 4 * i + j : 9 + 4 * i + j] = line

    r = row_index((2 * LANES, LANES))
    l = lane_index((2 * LANES, LANES))
    compact[...] = jnp.where((l < PAIR * 16) & (l % 16 == r // 16), 1.0, 0.0).astype(bf16)
    r = row_index((LANES, 2 * LANES))
    l = lane_index((LANES, 2 * LANES))
    expand[...] = jnp.where(r % 16 == l // 16, 1.0, 0.0).astype(bf16)
    fold = jnp.where(
        row_index((LANES, LANES)) % 16 == lane_index((LANES, LANES)) % 16, 1.0, 0.0
    ).astype(bf16)

    def info_copies():
        return [
            pltpu.make_async_remote_copy(
                src_ref=info, dst_ref=info_in.at[i], send_sem=info_send.at[i],
                recv_sem=info_recv.at[i], device_id=peer(*d), device_id_type=MESH,
            )
            for i, d in enumerate(ABOVE)
        ]

    def side_copies(n, g):
        fields = pl.ds(PAIR * g, PAIR)
        copies = []
        for k, d in enumerate(SIDES):
            if k == 0:
                src, dst = term.at[n, fields, pl.ds(CELL, 2)], term.at[n, fields, pl.ds(0, 2)]
            elif k == 1:
                src, dst = term.at[n, fields, pl.ds(2, 2)], term.at[n, fields, pl.ds(CELL + 2, 2)]
            else:
                rows = pl.ds(CELL - 2, 2) if k == 2 else pl.ds(0, 2)
                src, dst = term.at[n, fields, inner, rows], side_y.at[n, fields, :, rows]
            copies.append(
                pltpu.make_async_remote_copy(
                    src_ref=src, dst_ref=dst, send_sem=side_send.at[n, g, k],
                    recv_sem=side_recv.at[n, g, k], device_id=peer(*d), device_id_type=MESH,
                )
            )
        return copies

    def share_copies(n, g):
        return [
            pltpu.make_async_remote_copy(
                src_ref=shares_out.at[n, g, k], dst_ref=shares_in.at[n, g, k],
                send_sem=share_send.at[n, g, k], recv_sem=share_recv.at[n, g, k],
                device_id=peer(*d), device_id_type=MESH,
            )
            for k, d in enumerate(NEAR)
        ]

    pl.semaphore_wait(barrier, len(NEAR) + 1)

    for copy in info_copies():
        copy.start()
    for copy in load_fields:
        copy.wait()
    for g in range(2):
        for copy in side_copies(0, g):
            copy.start()

    load_table.wait()
    own_group = row_index((8, LANES)) == lane_index((8, LANES)) // 16
    for j in range(NPROJ):
        pieces = []
        for c in range(2 * BOX):
            line = table[j : j + 1, c * LANES : (c + 1) * LANES]
            pieces.append(jnp.where(own_group, jnp.broadcast_to(line, (8, LANES)), 0.0))
        boxes[j] = dot_exact(jnp.concatenate(pieces, axis=0), fold).reshape(BOX, BOX, LANES)

    def split_first(x, _):
        for f in range(FIELDS):
            high, low = halves(term[0, f, x + 2])
            split_term[f, x, :, :LANES] = high
            split_term[f, x, :, LANES:] = low
        return 0

    lax.fori_loop(0, CELL, split_first, 0)
    load_potential.wait()

    for copy in info_copies():
        copy.wait_recv()

    upper = lane >= 64
    from_xy, from_x, from_y = (info_in.at[i] for i in range(3))
    near_x = []
    for h in range(2):
        a, b = (info, from_x) if h == 0 else (from_y, from_xy)
        near_x.append(jnp.where(upper, b[...], a[...]))
    for h in range(2):
        depth = (near_x[h][2:3].astype(jnp.int32) + lane % 16) % LANES
        hit = row_index((LANES, LANES)) == depth
        pick = jnp.where(hit, 1.0, 0.0)
        across = pick.T.astype(bf16)
        pick = pick.astype(bf16)
        pick_in[:LANES, h * LANES : (h + 1) * LANES] = pick
        pick_in[LANES:, h * LANES : (h + 1) * LANES] = pick
        pick_out[h * LANES : (h + 1) * LANES] = across
        pick_out[(h + 2) * LANES : (h + 3) * LANES] = across
        for i in range(NPROJ):
            rows = near_x[h][8 + 4 * i : 12 + 4 * i]
            coupled[i, :, h * LANES : (h + 1) * LANES] = jnp.concatenate([rows] * PAIR, axis=0)

    row = row_index((CELL, LANES))
    for h in range(2):
        at_y = near_x[h][1:2].astype(jnp.int32)
        shift = jnp.broadcast_to(at_y if h == 0 else CELL - at_y, (CELL, LANES))
        bits = []
        for b in range(4):
            step = 1 << b
            stays = row >= step if h == 0 else row < CELL - step
            moved = (shift // step) % 2 == 1
            bits.append((step if h == 0 else CELL - step, moved & stays, moved & ~stays))
        whole = shift >= CELL

        def place_y(i, _, bits=bits, whole=whole, h=h):
            for j in range(NPROJ):
                v = boxes[j, i]
                for step, keep, drop in bits:
                    rolled = pltpu.roll(v, step, 0)
                    v = jnp.where(keep, rolled, jnp.where(drop, 0.0, v))
                placed_y[h, j, i] = jnp.where(whole, 0.0, v)
            return 0

        lax.fori_loop(0, BOX, place_y, 0)

    for h in range(2):
        at_x = jnp.broadcast_to(near_x[h][0:1].astype(jnp.int32), (CELL, LANES))
        above = jnp.broadcast_to(upper, (CELL, LANES))
        down = [~above & ((at_x // (1 << b)) % 2 == 1) for b in range(4)]
        up = [above & (((CELL - at_x) // (1 << b)) % 2 == 1) for b in range(4)]
        whole = above & (at_x == 0)

        def place_x(j, _, down=down, up=up, whole=whole, h=h):
            v = [placed_y[h, j, i] for i in range(BOX)]
            zero = jnp.zeros((CELL, LANES), f32)
            for b in range(4):
                step = 1 << b
                v = [
                    jnp.where(
                        down[b],
                        v[x - step] if x >= step else zero,
                        jnp.where(up[b], v[x + step] if x + step < CELL else zero, v[x]),
                    )
                    for x in range(CELL)
                ]
            for x in range(CELL):
                frames[h, j, x] = jnp.where(whole, 0.0, v[x])
            return 0

        lax.fori_loop(0, NPROJ, place_x, 0)

    def send_shares(n, q, g):
        cells = split_term[pl.ds(PAIR * g, PAIR)].reshape(PAIR * CELL * CELL, 2 * LANES)
        slabs[...] = jnp.dot(cells, pick_in[...], preferred_element_type=f32).reshape(slabs.shape)
        sums = []
        for h in range(2):

            def add(x, totals, h=h):
                frame = [frames[h, j, x] for j in range(NPROJ)]
                new = []
                for o in range(PAIR):
                    part = slabs[o, x, :, h * LANES : (h + 1) * LANES]
                    for j in range(NPROJ):
                        product = part * frame[j]
                        new.append(totals[o * NPROJ + j] + product[:8] + product[8:])
                return tuple(new)

            zero = jnp.zeros((8, LANES), f32)
            totals = lax.fori_loop(0, CELL, add, (zero,) * (PAIR * NPROJ), unroll=UNROLL)
            sums.append(jnp.concatenate([jnp.sum(t, axis=0, keepdims=True) for t in totals], axis=0))
        lines = dot_exact(jnp.concatenate(sums, axis=1), compact[...])
        mine = jnp.zeros((NPROJ, LANES), f32)
        lane4 = lane_index((NPROJ, LANES))
        for o in range(PAIR):
            mine = mine + jnp.where(lane4 // 16 == o, lines[4 * o : 4 * o + 4], 0.0)
        shares[q] = mine
        slot = (lane4 // 4) % 4
        valid = lane4 < PAIR * 16
        for k, (dx, dy) in enumerate(NEAR):
            keep = valid
            if dx:
                keep = keep & (slot % 2 == (1 if dx == 1 else 0))
            if dy:
                keep = keep & (slot // 2 == (1 if dy == 1 else 0))
            moved = pltpu.roll(mine, (4 * dx + 8 * dy) % LANES, 1)
            shares_out[n, g, k] = jnp.where(keep, moved, 0.0)
        for copy in share_copies(n, g):
            copy.start()

    for q in range(2):
        send_shares(0, q, q)

    row16 = row_index((CELL, LANES))

    def make_term(n, q, g, store):
        last, other = n - 1, 1 - g
        for copy in side_copies(last, other):
            copy.wait_recv()

        def stencil(x, _):
            v = pot[x]
            for o in range(PAIR):
                f = PAIR * other + o
                u = term[last, f, x + 2]
                edge = side_y[last, f, x]
                near = term[last, f, x + 1] + term[last, f, x + 3]
                far = term[last, f, x] + term[last, f, x + 4]
                near = near + pltpu.roll(jnp.where(row16 == 0, edge, u), CELL - 1, 0)
                near = near + pltpu.roll(jnp.where(row16 == CELL - 1, edge, u), 1, 0)
                far = far + pltpu.roll(jnp.where(row16 < 2, edge, u), CELL - 2, 0)
                far = far + pltpu.roll(jnp.where(row16 >= CELL - 2, edge, u), 2, 0)
                near = near + pltpu.roll(u, 1, 1) + pltpu.roll(u, LANES - 1, 1)
                far = far + pltpu.roll(u, 2, 1) + pltpu.roll(u, LANES - 2, 1)
                local_part[o, x] = (v + 3.75) * u + (-2.0 / 3.0) * near + (1.0 / 24.0) * far
            return 0

        lax.fori_loop(0, CELL, stencil, 0, unroll=UNROLL)

        for copy in share_copies(last, other):
            copy.wait_recv()
        total = shares[q]
        for k in range(len(NEAR)):
            total = total + shares_in[last, other, k]
        rows = PAIR * NPROJ
        field_of_row = row_index((rows, LANES)) // NPROJ
        field_of_lane = lane_index((rows, LANES)) // 16
        lines = [
            jnp.where(
                field_of_row == field_of_lane, jnp.broadcast_to(total[i : i + 1], (rows, LANES)), 0.0
            )
            for i in range(NPROJ)
        ]
        wide = dot_exact(jnp.concatenate(lines, axis=0), expand[...])
        weights = coupled[0] * wide[:rows]
        for i in range(1, NPROJ):
            weights = weights + coupled[i] * wide[i * rows : (i + 1) * rows]
        coef[...] = weights

        for h in range(2):
            lanes = pl.ds(h * LANES, LANES)

            def spread(x, _, h=h, lanes=lanes):
                frame = [frames[h, j, x] for j in range(NPROJ)]
                for o in range(PAIR):
                    value = coef[o * NPROJ : o * NPROJ + 1, lanes] * frame[0]
                    for j in range(1, NPROJ):
                        value = value + coef[o * NPROJ + j : o * NPROJ + j + 1, lanes] * frame[j]
                    high, low = halves(value)
                    split_values[o, x, :, h * LANES : (h + 1) * LANES] = high
                    split_values[o, x, :, (h + 2) * LANES : (h + 3) * LANES] = low
                return 0

            lax.fori_loop(0, CELL, spread, 0, unroll=UNROLL)

        projected[...] = jnp.dot(
            split_values[...].reshape(PAIR * CELL * CELL, 4 * LANES), pick_out[...],
            preferred_element_type=f32,
        ).reshape(projected.shape)
        factor = TIME_STEP / (jnp.zeros((CELL, LANES), f32) + n) * (1 - 2 * g)

        def line(x, _):
            for o in range(PAIR):
                store(PAIR * g + o, x, factor * (local_part[o, x] + projected[o, x]))
            return 0

        lax.fori_loop(0, CELL, line, 0, unroll=UNROLL)

    def step(m, _):
        n, q = m // 2, m % 2
        g = (n + q) % 2

        def store(f, x, value):
            term[n, f, x + 2] = value
            high, low = halves(value)
            split_term[f, x, :, :LANES] = high
            split_term[f, x, :, LANES:] = low

        make_term(n, q, g, store)
        for copy in side_copies(n, g):
            copy.start()
        send_shares(n, q, g)
        return 0

    lax.fori_loop(2, 2 * STEPS, step, 0)

    def store_last(f, x, value):
        total = term[0, f, x + 2] + term[1, f, x + 2]
        propagated_ref[f, x] = total + term[2, f, x + 2] + term[3, f, x + 2] + value

    def finish(q, _):
        make_term(STEPS, q, q, store_last)
        return 0

    lax.fori_loop(0, 2, finish, 0)

    occupied = [jnp.broadcast_to(occupations_ref[0:1, o : o + 1], (CELL, LANES)) for o in range(PAIR)]

    def density(x, _):
        total = jnp.zeros((CELL, LANES), f32)
        for f in range(FIELDS):
            total = total + occupied[f % PAIR] * (propagated_ref[f, x] * propagated_ref[f, x])
        dens[x] = total
        return 0

    lax.fori_loop(0, CELL, density, 0, unroll=UNROLL)
    send = pltpu.make_async_remote_copy(
        src_ref=dens, dst_ref=dens_in, send_sem=dens_send, recv_sem=dens_recv,
        device_id=partner(), device_id_type=MESH,
    )
    send.start()
    for copy in info_copies():
        copy.wait_send()

    def drain(n, _):
        for g in range(2):
            for copy in side_copies(n, g) + share_copies(n, g):
                copy.wait_send()
        return 0

    lax.fori_loop(0, STEPS, drain, 0)
    send.wait_recv()
    density_ref[...] = dens[...] + dens_in[...]
    send.wait_send()


def hand_over(propagated_ref, density_ref, propagated_out, density_out, sem):
    copies = [
        pltpu.make_async_copy(propagated_ref.at[f], propagated_out.at[f], sem.at[f])
        for f in range(FIELDS)
    ]
    copies.append(pltpu.make_async_copy(density_ref, density_out, sem.at[FIELDS]))
    for copy in copies:
        copy.start()
    for copy in copies:
        copy.wait()


def local(orbitals, potential, corners, counts, coupling, projectors, occupations):
    fields = orbitals.reshape(FIELDS, CELL, CELL, LANES)
    vmem = pl.BlockSpec(memory_space=pltpu.VMEM)
    hbm = pl.BlockSpec(memory_space=pltpu.HBM)
    grid = (CELL, CELL, LANES)
    dma = pltpu.SemaphoreType.DMA
    near = len(NEAR)
    propagated, density = pl.pallas_call(
        kernel,
        out_shape=(
            pltpu.VMEM((FIELDS,) + grid, f32),
            pltpu.VMEM(grid, f32),
        ),
        in_specs=[hbm] * 7,
        out_specs=(vmem, vmem),
        scratch_shapes=[
            pltpu.VMEM((STEPS, FIELDS, CELL + 4, CELL, LANES), f32),
            pltpu.VMEM((STEPS, FIELDS) + grid, f32),
            pltpu.VMEM((PAIR,) + grid, f32),
            pltpu.VMEM(grid, f32),
            pltpu.VMEM((NPROJ, BOX * BOX * BOX), f32),
            pltpu.VMEM((4, 3), jnp.int32),
            pltpu.VMEM((1, 4), jnp.int32),
            pltpu.VMEM((4, NPROJ, NPROJ), f32),
            pltpu.VMEM((1, PAIR), f32),
            pltpu.VMEM((24, LANES), f32),
            pltpu.VMEM((3, 24, LANES), f32),
            pltpu.VMEM((NPROJ,) + grid, f32),
            pltpu.VMEM((2, NPROJ) + grid, f32),
            pltpu.VMEM((2, NPROJ) + grid, f32),
            pltpu.VMEM((2 * LANES, 2 * LANES), bf16),
            pltpu.VMEM((4 * LANES, LANES), bf16),
            pltpu.VMEM((2 * LANES, LANES), bf16),
            pltpu.VMEM((LANES, 2 * LANES), bf16),
            pltpu.VMEM((NPROJ, PAIR * NPROJ, 2 * LANES), f32),
            pltpu.VMEM((PAIR * NPROJ, 2 * LANES), f32),
            pltpu.VMEM((FIELDS, CELL, CELL, 2 * LANES), bf16),
            pltpu.VMEM((PAIR, CELL, CELL, 2 * LANES), f32),
            pltpu.VMEM((PAIR, CELL, CELL, 4 * LANES), bf16),
            pltpu.VMEM((PAIR,) + grid, f32),
            pltpu.VMEM((2, NPROJ, LANES), f32),
            pltpu.VMEM((STEPS, 2, near, NPROJ, LANES), f32),
            pltpu.VMEM((STEPS, 2, near, NPROJ, LANES), f32),
            pltpu.VMEM(grid, f32),
            pltpu.VMEM(grid, f32),
            dma((FIELDS + 6,)),
            dma((3,)),
            dma((3,)),
            dma((STEPS, 2, 4)),
            dma((STEPS, 2, 4)),
            dma((STEPS, 2, near)),
            dma((STEPS, 2, near)),
            dma,
            dma,
        ],
        compiler_params=pltpu.CompilerParams(
            collective_id=1, has_side_effects=True, vmem_limit_bytes=VMEM_BYTES
        ),
    )(
        fields, potential, corners, counts[None], coupling, projectors, occupations[None]
    )
    return propagated.reshape(orbitals.shape), density


def solution(mesh):
    placed = (
        P(None, "band", "gx", "gy", None),
        P("gx", "gy", None),
        P(("gx", "gy"), None),
        P(("gx", "gy")),
        P(("gx", "gy"), None, None),
        P(),
        P("band"),
    )
    return jax.shard_map(
        local,
        mesh=mesh,
        in_specs=placed,
        out_specs=(P(None, "band", "gx", "gy", None), P("gx", "gy", None)),
        check_vma=False,
    )
```

```python
import jax
import jax.numpy as jnp
from jax import lax
from jax.experimental import pallas as pl
from jax.experimental.pallas import tpu as pltpu
from jax.sharding import PartitionSpec as P

BOX = 16
NPROJ = 4
CELL = 16
LANES = 128
FIELDS = 4
STEPS = 4
PAIR = 2
UNROLL = 16
VMEM_BYTES = 60 * 2**20
TIME_STEP = 0.12
MESH = pl.DeviceIdType.MESH
f32 = jnp.float32
bf16 = jnp.bfloat16

NEAR = tuple((dx, dy) for dx in (-1, 1, 0) for dy in (-1, 1, 0) if (dx, dy) != (0, 0))
ABOVE = ((1, 1), (1, 0), (0, 1))
SIDES = ((1, 0), (-1, 0), (0, 1), (0, -1))


def peer(step_x, step_y):
    size_x, size_y = lax.axis_size("gx"), lax.axis_size("gy")
    return (
        lax.rem(lax.axis_index("gx") + step_x + size_x, size_x),
        lax.rem(lax.axis_index("gy") + step_y + size_y, size_y),
        lax.axis_index("band"),
    )


def partner():
    return (lax.axis_index("gx"), lax.axis_index("gy"), 1 - lax.axis_index("band"))


def lane_index(shape):
    return lax.broadcasted_iota(jnp.int32, shape, len(shape) - 1)


def row_index(shape):
    return lax.broadcasted_iota(jnp.int32, shape, len(shape) - 2)


def halves(x):
    high = x.astype(bf16)
    low = (x - high.astype(f32)).astype(bf16)
    return high, low


def thirds(x):
    high = x.astype(bf16)
    rest = x - high.astype(f32)
    mid = rest.astype(bf16)
    low = (rest - mid.astype(f32)).astype(bf16)
    return high, mid, low


def dot_exact(x, pick):
    rows = x.shape[0]
    r = jnp.dot(jnp.concatenate(thirds(x), axis=0), pick, preferred_element_type=f32)
    return r[:rows] + r[rows : 2 * rows] + r[2 * rows :]


def kernel(
    fields_ref, potential_ref, corners_hbm, counts_hbm, coupling_hbm, projectors_ref, occupations_hbm,
    propagated_ref, density_ref,
    term, side_y, local_part, pot, table, corners_ref, counts_ref, coupling_ref, occupations_ref, info, info_in, boxes, placed_y, frames,
    pick_in, pick_out, compact, expand, coupled, coef, split_term, slabs, split_values, projected,
    shares, shares_out, shares_in, dens, dens_in,
    load_sem, info_send, info_recv, side_send, side_recv, share_send, share_recv,
    dens_send, dens_recv,
):
    inner = pl.ds(2, CELL)

    barrier = pltpu.get_barrier_semaphore()
    for d in NEAR:
        pl.semaphore_signal(barrier, inc=1, device_id=peer(*d), device_id_type=MESH)
    pl.semaphore_signal(barrier, inc=1, device_id=partner(), device_id_type=MESH)

    load_fields = [
        pltpu.make_async_copy(fields_ref.at[f], term.at[0, f, inner], load_sem.at[f])
        for f in range(FIELDS)
    ]
    load_potential = pltpu.make_async_copy(potential_ref, pot, load_sem.at[FIELDS])
    load_table = pltpu.make_async_copy(projectors_ref, table, load_sem.at[FIELDS + 1])
    load_atoms = [
        pltpu.make_async_copy(src, dst, load_sem.at[FIELDS + 2 + i])
        for i, (src, dst) in enumerate(
            (
                (corners_hbm, corners_ref),
                (counts_hbm, counts_ref),
                (coupling_hbm, coupling_ref),
                (occupations_hbm, occupations_ref),
            )
        )
    ]
    for copy in load_atoms:
        copy.start()
    load_table.start()
    for copy in load_fields:
        copy.start()
    load_potential.start()

    lane = lane_index((1, LANES))
    atom_of_lane = (lane // BOX) % 4

    for copy in load_atoms:
        copy.wait()

    def over_atoms(values):
        values = [jnp.broadcast_to(v, (1, LANES)) for v in values]
        line = jnp.where(atom_of_lane == 0, values[0], values[1])
        line = jnp.where(atom_of_lane == 2, values[2], line)
        return jnp.where(atom_of_lane == 3, values[3], line)

    for axis in range(3):
        line = over_atoms([corners_ref[a : a + 1, axis : axis + 1] for a in range(4)])
        line = line % CELL if axis < 2 else line
        info[axis : axis + 1] = line.astype(f32)
    count = over_atoms([counts_ref[0:1, a : a + 1] for a in range(4)])
    entry = [
        [over_atoms([coupling_ref[a, j : j + 1, i : i + 1] for a in range(4)]) for i in range(NPROJ)]
        for j in range(NPROJ)
    ]
    for i in range(NPROJ):
        for j in range(NPROJ):
            line = jnp.where(count > max(i, j), 0.5 * (entry[j][i] + entry[i][j]), 0.0)
            info[8 + 4 * i + j : 9 + 4 * i + j] = line

    r = row_index((2 * LANES, LANES))
    l = lane_index((2 * LANES, LANES))
    compact[...] = jnp.where((l < PAIR * 16) & (l % 16 == r // 16), 1.0, 0.0).astype(bf16)
    r = row_index((LANES, 2 * LANES))
    l = lane_index((LANES, 2 * LANES))
    expand[...] = jnp.where(r % 16 == l // 16, 1.0, 0.0).astype(bf16)
    fold = jnp.where(
        row_index((LANES, LANES)) % 16 == lane_index((LANES, LANES)) % 16, 1.0, 0.0
    ).astype(bf16)

    def info_copies():
        return [
            pltpu.make_async_remote_copy(
                src_ref=info, dst_ref=info_in.at[i], send_sem=info_send.at[i],
                recv_sem=info_recv.at[i], device_id=peer(*d), device_id_type=MESH,
            )
            for i, d in enumerate(ABOVE)
        ]

    def side_copies(n, g):
        fields = pl.ds(PAIR * g, PAIR)
        copies = []
        for k, d in enumerate(SIDES):
            if k == 0:
                src, dst = term.at[n, fields, pl.ds(CELL, 2)], term.at[n, fields, pl.ds(0, 2)]
            elif k == 1:
                src, dst = term.at[n, fields, pl.ds(2, 2)], term.at[n, fields, pl.ds(CELL + 2, 2)]
            else:
                rows = pl.ds(CELL - 2, 2) if k == 2 else pl.ds(0, 2)
                src, dst = term.at[n, fields, inner, rows], side_y.at[n, fields, :, rows]
            copies.append(
                pltpu.make_async_remote_copy(
                    src_ref=src, dst_ref=dst, send_sem=side_send.at[n, g, k],
                    recv_sem=side_recv.at[n, g, k], device_id=peer(*d), device_id_type=MESH,
                )
            )
        return copies

    def share_copies(n, g):
        return [
            pltpu.make_async_remote_copy(
                src_ref=shares_out.at[n, g, k], dst_ref=shares_in.at[n, g, k],
                send_sem=share_send.at[n, g, k], recv_sem=share_recv.at[n, g, k],
                device_id=peer(*d), device_id_type=MESH,
            )
            for k, d in enumerate(NEAR)
        ]

    pl.semaphore_wait(barrier, len(NEAR) + 1)

    for copy in info_copies():
        copy.start()
    for copy in load_fields:
        copy.wait()
    for g in range(2):
        for copy in side_copies(0, g):
            copy.start()

    load_table.wait()
    own_group = row_index((8, LANES)) == lane_index((8, LANES)) // 16
    for j in range(NPROJ):
        pieces = []
        for c in range(2 * BOX):
            line = table[j : j + 1, c * LANES : (c + 1) * LANES]
            pieces.append(jnp.where(own_group, jnp.broadcast_to(line, (8, LANES)), 0.0))
        boxes[j] = dot_exact(jnp.concatenate(pieces, axis=0), fold).reshape(BOX, BOX, LANES)

    def split_first(x, _):
        for f in range(FIELDS):
            high, low = halves(term[0, f, x + 2])
            split_term[f, x, :, :LANES] = high
            split_term[f, x, :, LANES:] = low
        return 0

    lax.fori_loop(0, CELL, split_first, 0, unroll=UNROLL)
    load_potential.wait()

    for copy in info_copies():
        copy.wait_recv()

    upper = lane >= 64
    from_xy, from_x, from_y = (info_in.at[i] for i in range(3))
    near_x = []
    for h in range(2):
        a, b = (info, from_x) if h == 0 else (from_y, from_xy)
        near_x.append(jnp.where(upper, b[...], a[...]))
    for h in range(2):
        depth = (near_x[h][2:3].astype(jnp.int32) + lane % 16) % LANES
        hit = row_index((LANES, LANES)) == depth
        pick = jnp.where(hit, 1.0, 0.0)
        across = pick.T.astype(bf16)
        pick = pick.astype(bf16)
        pick_in[:LANES, h * LANES : (h + 1) * LANES] = pick
        pick_in[LANES:, h * LANES : (h + 1) * LANES] = pick
        pick_out[h * LANES : (h + 1) * LANES] = across
        pick_out[(h + 2) * LANES : (h + 3) * LANES] = across
        for i in range(NPROJ):
            rows = near_x[h][8 + 4 * i : 12 + 4 * i]
            coupled[i, :, h * LANES : (h + 1) * LANES] = jnp.concatenate([rows] * PAIR, axis=0)

    row = row_index((CELL, LANES))
    for h in range(2):
        at_y = near_x[h][1:2].astype(jnp.int32)
        shift = jnp.broadcast_to(at_y if h == 0 else CELL - at_y, (CELL, LANES))
        bits = []
        for b in range(4):
            step = 1 << b
            stays = row >= step if h == 0 else row < CELL - step
            moved = (shift // step) % 2 == 1
            bits.append((step if h == 0 else CELL - step, moved & stays, moved & ~stays))
        whole = shift >= CELL

        def place_y(i, _, bits=bits, whole=whole, h=h):
            for j in range(NPROJ):
                v = boxes[j, i]
                for step, keep, drop in bits:
                    rolled = pltpu.roll(v, step, 0)
                    v = jnp.where(keep, rolled, jnp.where(drop, 0.0, v))
                placed_y[h, j, i] = jnp.where(whole, 0.0, v)
            return 0

        lax.fori_loop(0, BOX, place_y, 0, unroll=UNROLL)

    for h in range(2):
        at_x = jnp.broadcast_to(near_x[h][0:1].astype(jnp.int32), (CELL, LANES))
        above = jnp.broadcast_to(upper, (CELL, LANES))
        down = [~above & ((at_x // (1 << b)) % 2 == 1) for b in range(4)]
        up = [above & (((CELL - at_x) // (1 << b)) % 2 == 1) for b in range(4)]
        whole = above & (at_x == 0)

        def place_x(j, _, down=down, up=up, whole=whole, h=h):
            v = [placed_y[h, j, i] for i in range(BOX)]
            zero = jnp.zeros((CELL, LANES), f32)
            for b in range(4):
                step = 1 << b
                v = [
                    jnp.where(
                        down[b],
                        v[x - step] if x >= step else zero,
                        jnp.where(up[b], v[x + step] if x + step < CELL else zero, v[x]),
                    )
                    for x in range(CELL)
                ]
            for x in range(CELL):
                frames[h, j, x] = jnp.where(whole, 0.0, v[x])
            return 0

        lax.fori_loop(0, NPROJ, place_x, 0, unroll=NPROJ)

    def send_shares(n, q, g):
        cells = split_term[pl.ds(PAIR * g, PAIR)].reshape(PAIR * CELL * CELL, 2 * LANES)
        slabs[...] = jnp.dot(cells, pick_in[...], preferred_element_type=f32).reshape(slabs.shape)
        sums = []
        for h in range(2):

            def add(x, totals, h=h):
                frame = [frames[h, j, x] for j in range(NPROJ)]
                new = []
                for o in range(PAIR):
                    part = slabs[o, x, :, h * LANES : (h + 1) * LANES]
                    for j in range(NPROJ):
                        product = part * frame[j]
                        new.append(totals[o * NPROJ + j] + product[:8] + product[8:])
                return tuple(new)

            zero = jnp.zeros((8, LANES), f32)
            totals = lax.fori_loop(0, CELL, add, (zero,) * (PAIR * NPROJ), unroll=UNROLL)
            sums.append(jnp.concatenate([jnp.sum(t, axis=0, keepdims=True) for t in totals], axis=0))
        lines = dot_exact(jnp.concatenate(sums, axis=1), compact[...])
        mine = jnp.zeros((NPROJ, LANES), f32)
        lane4 = lane_index((NPROJ, LANES))
        for o in range(PAIR):
            mine = mine + jnp.where(lane4 // 16 == o, lines[4 * o : 4 * o + 4], 0.0)
        shares[q] = mine
        slot = (lane4 // 4) % 4
        valid = lane4 < PAIR * 16
        for k, (dx, dy) in enumerate(NEAR):
            keep = valid
            if dx:
                keep = keep & (slot % 2 == (1 if dx == 1 else 0))
            if dy:
                keep = keep & (slot // 2 == (1 if dy == 1 else 0))
            moved = pltpu.roll(mine, (4 * dx + 8 * dy) % LANES, 1)
            shares_out[n, g, k] = jnp.where(keep, moved, 0.0)
        for copy in share_copies(n, g):
            copy.start()

    for q in range(2):
        send_shares(0, q, q)

    row16 = row_index((CELL, LANES))

    def make_term(n, q, g, store, spans=((0, CELL),), after=None):
        last, other = n - 1, 1 - g
        for copy in side_copies(last, other):
            copy.wait_recv()

        def stencil(x, _):
            v = pot[x]
            for o in range(PAIR):
                f = PAIR * other + o
                u = term[last, f, x + 2]
                edge = side_y[last, f, x]
                near = term[last, f, x + 1] + term[last, f, x + 3]
                far = term[last, f, x] + term[last, f, x + 4]
                near = near + pltpu.roll(jnp.where(row16 == 0, edge, u), CELL - 1, 0)
                near = near + pltpu.roll(jnp.where(row16 == CELL - 1, edge, u), 1, 0)
                far = far + pltpu.roll(jnp.where(row16 < 2, edge, u), CELL - 2, 0)
                far = far + pltpu.roll(jnp.where(row16 >= CELL - 2, edge, u), 2, 0)
                near = near + pltpu.roll(u, 1, 1) + pltpu.roll(u, LANES - 1, 1)
                far = far + pltpu.roll(u, 2, 1) + pltpu.roll(u, LANES - 2, 1)
                local_part[o, x] = (v + 3.75) * u + (-2.0 / 3.0) * near + (1.0 / 24.0) * far
            return 0

        lax.fori_loop(0, CELL, stencil, 0, unroll=UNROLL)

        for copy in share_copies(last, other):
            copy.wait_recv()
        total = shares[q]
        for k in range(len(NEAR)):
            total = total + shares_in[last, other, k]
        rows = PAIR * NPROJ
        field_of_row = row_index((rows, LANES)) // NPROJ
        field_of_lane = lane_index((rows, LANES)) // 16
        lines = [
            jnp.where(
                field_of_row == field_of_lane, jnp.broadcast_to(total[i : i + 1], (rows, LANES)), 0.0
            )
            for i in range(NPROJ)
        ]
        wide = dot_exact(jnp.concatenate(lines, axis=0), expand[...])
        weights = coupled[0] * wide[:rows]
        for i in range(1, NPROJ):
            weights = weights + coupled[i] * wide[i * rows : (i + 1) * rows]
        coef[...] = weights

        factor = TIME_STEP / (jnp.zeros((CELL, LANES), f32) + n) * (1 - 2 * g)

        def spread(x, _):
            for h in range(2):
                lanes = pl.ds(h * LANES, LANES)
                frame = [frames[h, j, x] for j in range(NPROJ)]
                for o in range(PAIR):
                    value = coef[o * NPROJ : o * NPROJ + 1, lanes] * frame[0]
                    for j in range(1, NPROJ):
                        value = value + coef[o * NPROJ + j : o * NPROJ + j + 1, lanes] * frame[j]
                    high, low = halves(value)
                    split_values[o, x, :, h * LANES : (h + 1) * LANES] = high
                    split_values[o, x, :, (h + 2) * LANES : (h + 3) * LANES] = low
            return 0

        def line(x, _):
            for o in range(PAIR):
                store(PAIR * g + o, x, factor * (local_part[o, x] + projected[o, x]))
            return 0

        for first, end in spans:
            count = end - first
            lax.fori_loop(first, end, spread, 0, unroll=count)
            part = split_values[:, first:end].reshape(PAIR * count * CELL, 4 * LANES)
            projected[:, first:end] = jnp.dot(
                part, pick_out[...], preferred_element_type=f32
            ).reshape(PAIR, count, CELL, LANES)
            lax.fori_loop(first, end, line, 0, unroll=count)
            if after is not None:
                after(first, end)

    def step(m, _):
        n, q = m // 2, m % 2
        g = (n + q) % 2

        def store(f, x, value):
            term[n, f, x + 2] = value
            high, low = halves(value)
            split_term[f, x, :, :LANES] = high
            split_term[f, x, :, LANES:] = low

        make_term(n, q, g, store)
        for copy in side_copies(n, g):
            copy.start()
        send_shares(n, q, g)
        return 0

    lax.fori_loop(2, 2 * STEPS, step, 0)

    def store_last(f, x, value):
        total = term[0, f, x + 2] + term[1, f, x + 2]
        propagated_ref[f, x] = total + term[2, f, x + 2] + term[3, f, x + 2] + value

    occupied = [jnp.broadcast_to(occupations_ref[0:1, o : o + 1], (CELL, LANES)) for o in range(PAIR)]
    middle = CELL // 2

    def density_copy(i):
        half = pl.ds(i * middle, middle)
        return pltpu.make_async_remote_copy(
            src_ref=dens.at[half], dst_ref=dens_in.at[half], send_sem=dens_send.at[i],
            recv_sem=dens_recv.at[i], device_id=partner(), device_id_type=MESH,
        )

    def send_density(first, end):
        def density(x, _):
            total = jnp.zeros((CELL, LANES), f32)
            for f in range(FIELDS):
                total = total + occupied[f % PAIR] * (propagated_ref[f, x] * propagated_ref[f, x])
            dens[x] = total
            return 0

        lax.fori_loop(first, end, density, 0, unroll=end - first)
        density_copy(first // middle).start()

    make_term(STEPS, 0, 0, store_last)
    make_term(STEPS, 1, 1, store_last, ((0, middle), (middle, CELL)), send_density)
    for copy in info_copies():
        copy.wait_send()

    def drain(n, _):
        for g in range(2):
            for copy in side_copies(n, g) + share_copies(n, g):
                copy.wait_send()
        return 0

    lax.fori_loop(0, STEPS, drain, 0)
    for i in range(2):
        density_copy(i).wait_recv()
        half = pl.ds(i * middle, middle)
        density_ref[half] = dens[half] + dens_in[half]
    for i in range(2):
        density_copy(i).wait_send()


def hand_over(propagated_ref, density_ref, propagated_out, density_out, sem):
    copies = [
        pltpu.make_async_copy(propagated_ref.at[f], propagated_out.at[f], sem.at[f])
        for f in range(FIELDS)
    ]
    copies.append(pltpu.make_async_copy(density_ref, density_out, sem.at[FIELDS]))
    for copy in copies:
        copy.start()
    for copy in copies:
        copy.wait()


def local(orbitals, potential, corners, counts, coupling, projectors, occupations):
    fields = orbitals.reshape(FIELDS, CELL, CELL, LANES)
    vmem = pl.BlockSpec(memory_space=pltpu.VMEM)
    hbm = pl.BlockSpec(memory_space=pltpu.HBM)
    grid = (CELL, CELL, LANES)
    dma = pltpu.SemaphoreType.DMA
    near = len(NEAR)
    propagated, density = pl.pallas_call(
        kernel,
        out_shape=(
            pltpu.VMEM((FIELDS,) + grid, f32),
            pltpu.VMEM(grid, f32),
        ),
        in_specs=[hbm] * 7,
        out_specs=(vmem, vmem),
        scratch_shapes=[
            pltpu.VMEM((STEPS, FIELDS, CELL + 4, CELL, LANES), f32),
            pltpu.VMEM((STEPS, FIELDS) + grid, f32),
            pltpu.VMEM((PAIR,) + grid, f32),
            pltpu.VMEM(grid, f32),
            pltpu.VMEM((NPROJ, BOX * BOX * BOX), f32),
            pltpu.VMEM((4, 3), jnp.int32),
            pltpu.VMEM((1, 4), jnp.int32),
            pltpu.VMEM((4, NPROJ, NPROJ), f32),
            pltpu.VMEM((1, PAIR), f32),
            pltpu.VMEM((24, LANES), f32),
            pltpu.VMEM((3, 24, LANES), f32),
            pltpu.VMEM((NPROJ,) + grid, f32),
            pltpu.VMEM((2, NPROJ) + grid, f32),
            pltpu.VMEM((2, NPROJ) + grid, f32),
            pltpu.VMEM((2 * LANES, 2 * LANES), bf16),
            pltpu.VMEM((4 * LANES, LANES), bf16),
            pltpu.VMEM((2 * LANES, LANES), bf16),
            pltpu.VMEM((LANES, 2 * LANES), bf16),
            pltpu.VMEM((NPROJ, PAIR * NPROJ, 2 * LANES), f32),
            pltpu.VMEM((PAIR * NPROJ, 2 * LANES), f32),
            pltpu.VMEM((FIELDS, CELL, CELL, 2 * LANES), bf16),
            pltpu.VMEM((PAIR, CELL, CELL, 2 * LANES), f32),
            pltpu.VMEM((PAIR, CELL, CELL, 4 * LANES), bf16),
            pltpu.VMEM((PAIR,) + grid, f32),
            pltpu.VMEM((2, NPROJ, LANES), f32),
            pltpu.VMEM((STEPS, 2, near, NPROJ, LANES), f32),
            pltpu.VMEM((STEPS, 2, near, NPROJ, LANES), f32),
            pltpu.VMEM(grid, f32),
            pltpu.VMEM(grid, f32),
            dma((FIELDS + 6,)),
            dma((3,)),
            dma((3,)),
            dma((STEPS, 2, 4)),
            dma((STEPS, 2, 4)),
            dma((STEPS, 2, near)),
            dma((STEPS, 2, near)),
            dma((2,)),
            dma((2,)),
        ],
        compiler_params=pltpu.CompilerParams(
            collective_id=1, has_side_effects=True, vmem_limit_bytes=VMEM_BYTES
        ),
    )(
        fields, potential, corners, counts[None], coupling, projectors, occupations[None]
    )
    propagated, density = pl.pallas_call(
        hand_over,
        out_shape=(
            jax.ShapeDtypeStruct((FIELDS,) + grid, f32),
            jax.ShapeDtypeStruct(grid, f32),
        ),
        in_specs=[vmem] * 2,
        out_specs=(hbm, hbm),
        scratch_shapes=[dma((FIELDS + 1,))],
        compiler_params=pltpu.CompilerParams(vmem_limit_bytes=2**20),
    )(propagated, density)
    return propagated.reshape(orbitals.shape), density


def solution(mesh):
    placed = (
        P(None, "band", "gx", "gy", None),
        P("gx", "gy", None),
        P(("gx", "gy"), None),
        P(("gx", "gy")),
        P(("gx", "gy"), None, None),
        P(),
        P("band"),
    )
    return jax.shard_map(
        local,
        mesh=mesh,
        in_specs=placed,
        out_specs=(P(None, "band", "gx", "gy", None), P("gx", "gy", None)),
        check_vma=False,
    )
```

```python
import jax
import jax.numpy as jnp
from jax import lax
from jax.experimental import pallas as pl
from jax.experimental.pallas import tpu as pltpu
from jax.sharding import PartitionSpec as P

BOX = 16
NPROJ = 4
CELL = 16
LANES = 128
FIELDS = 4
STEPS = 4
PAIR = 2
UNROLL = 16
VMEM_BYTES = 60 * 2**20
TIME_STEP = 0.12
MESH = pl.DeviceIdType.MESH
f32 = jnp.float32
bf16 = jnp.bfloat16

NEAR = tuple((dx, dy) for dx in (-1, 1, 0) for dy in (-1, 1, 0) if (dx, dy) != (0, 0))
ABOVE = ((1, 1), (1, 0), (0, 1))
SIDES = ((1, 0), (-1, 0), (0, 1), (0, -1))


def peer(step_x, step_y):
    size_x, size_y = lax.axis_size("gx"), lax.axis_size("gy")
    return (
        lax.rem(lax.axis_index("gx") + step_x + size_x, size_x),
        lax.rem(lax.axis_index("gy") + step_y + size_y, size_y),
        lax.axis_index("band"),
    )


def partner():
    return (lax.axis_index("gx"), lax.axis_index("gy"), 1 - lax.axis_index("band"))


def lane_index(shape):
    return lax.broadcasted_iota(jnp.int32, shape, len(shape) - 1)


def row_index(shape):
    return lax.broadcasted_iota(jnp.int32, shape, len(shape) - 2)


def halves(x):
    high = x.astype(bf16)
    low = (x - high.astype(f32)).astype(bf16)
    return high, low


def thirds(x):
    high = x.astype(bf16)
    rest = x - high.astype(f32)
    mid = rest.astype(bf16)
    low = (rest - mid.astype(f32)).astype(bf16)
    return high, mid, low


def dot_exact(x, pick):
    rows = x.shape[0]
    r = jnp.dot(jnp.concatenate(thirds(x), axis=0), pick, preferred_element_type=f32)
    return r[:rows] + r[rows : 2 * rows] + r[2 * rows :]


def kernel(
    fields_ref, potential_ref, corners_hbm, counts_hbm, coupling_hbm, projectors_ref, occupations_hbm,
    propagated_ref, density_ref,
    term, side_y, local_part, pot, table, corners_ref, counts_ref, coupling_ref, occupations_ref, info, info_in, boxes, placed_y, frames,
    pick_in, pick_out, compact, expand, coupled, coef, split_term, slabs, split_values, projected,
    shares, shares_out, shares_in, dens, dens_in,
    load_sem, info_send, info_recv, side_send, side_recv, share_send, share_recv,
    dens_send, dens_recv,
):
    inner = pl.ds(2, CELL)

    barrier = pltpu.get_barrier_semaphore()
    for d in NEAR:
        pl.semaphore_signal(barrier, inc=1, device_id=peer(*d), device_id_type=MESH)
    pl.semaphore_signal(barrier, inc=1, device_id=partner(), device_id_type=MESH)

    load_fields = [
        pltpu.make_async_copy(fields_ref.at[f], term.at[0, f, inner], load_sem.at[f])
        for f in range(FIELDS)
    ]
    load_potential = pltpu.make_async_copy(potential_ref, pot, load_sem.at[FIELDS])
    load_table = pltpu.make_async_copy(projectors_ref, table, load_sem.at[FIELDS + 1])
    load_atoms = [
        pltpu.make_async_copy(src, dst, load_sem.at[FIELDS + 2 + i])
        for i, (src, dst) in enumerate(
            (
                (corners_hbm, corners_ref),
                (counts_hbm, counts_ref),
                (coupling_hbm, coupling_ref),
                (occupations_hbm, occupations_ref),
            )
        )
    ]
    for copy in load_atoms:
        copy.start()
    load_table.start()
    for copy in load_fields:
        copy.start()
    load_potential.start()

    lane = lane_index((1, LANES))
    atom_of_lane = (lane // BOX) % 4

    for copy in load_atoms:
        copy.wait()

    def over_atoms(values):
        values = [jnp.broadcast_to(v, (1, LANES)) for v in values]
        line = jnp.where(atom_of_lane == 0, values[0], values[1])
        line = jnp.where(atom_of_lane == 2, values[2], line)
        return jnp.where(atom_of_lane == 3, values[3], line)

    for axis in range(3):
        line = over_atoms([corners_ref[a : a + 1, axis : axis + 1] for a in range(4)])
        line = line % CELL if axis < 2 else line
        info[axis : axis + 1] = line.astype(f32)
    count = over_atoms([counts_ref[0:1, a : a + 1] for a in range(4)])
    entry = [
        [over_atoms([coupling_ref[a, j : j + 1, i : i + 1] for a in range(4)]) for i in range(NPROJ)]
        for j in range(NPROJ)
    ]
    for i in range(NPROJ):
        for j in range(NPROJ):
            line = jnp.where(count > max(i, j), 0.5 * (entry[j][i] + entry[i][j]), 0.0)
            info[8 + 4 * i + j : 9 + 4 * i + j] = line

    r = row_index((2 * LANES, LANES))
    l = lane_index((2 * LANES, LANES))
    compact[...] = jnp.where((l < PAIR * 16) & (l % 16 == r // 16), 1.0, 0.0).astype(bf16)
    r = row_index((LANES, 2 * LANES))
    l = lane_index((LANES, 2 * LANES))
    expand[...] = jnp.where(r % 16 == l // 16, 1.0, 0.0).astype(bf16)
    fold = jnp.where(
        row_index((LANES, LANES)) % 16 == lane_index((LANES, LANES)) % 16, 1.0, 0.0
    ).astype(bf16)

    def info_copies():
        return [
            pltpu.make_async_remote_copy(
                src_ref=info, dst_ref=info_in.at[i], send_sem=info_send.at[i],
                recv_sem=info_recv.at[i], device_id=peer(*d), device_id_type=MESH,
            )
            for i, d in enumerate(ABOVE)
        ]

    def side_copies(n, g):
        fields = pl.ds(PAIR * g, PAIR)
        copies = []
        for k, d in enumerate(SIDES):
            if k == 0:
                src, dst = term.at[n, fields, pl.ds(CELL, 2)], term.at[n, fields, pl.ds(0, 2)]
            elif k == 1:
                src, dst = term.at[n, fields, pl.ds(2, 2)], term.at[n, fields, pl.ds(CELL + 2, 2)]
            else:
                rows = pl.ds(CELL - 2, 2) if k == 2 else pl.ds(0, 2)
                src, dst = term.at[n, fields, inner, rows], side_y.at[n, fields, :, rows]
            copies.append(
                pltpu.make_async_remote_copy(
                    src_ref=src, dst_ref=dst, send_sem=side_send.at[n, g, k],
                    recv_sem=side_recv.at[n, g, k], device_id=peer(*d), device_id_type=MESH,
                )
            )
        return copies

    def share_copies(n, g):
        return [
            pltpu.make_async_remote_copy(
                src_ref=shares_out.at[n, g, k], dst_ref=shares_in.at[n, g, k],
                send_sem=share_send.at[n, g, k], recv_sem=share_recv.at[n, g, k],
                device_id=peer(*d), device_id_type=MESH,
            )
            for k, d in enumerate(NEAR)
        ]

    pl.semaphore_wait(barrier, len(NEAR) + 1)

    for copy in info_copies():
        copy.start()
    for copy in load_fields:
        copy.wait()
    for g in range(2):
        for copy in side_copies(0, g):
            copy.start()

    load_table.wait()
    own_group = row_index((8, LANES)) == lane_index((8, LANES)) // 16
    for j in range(NPROJ):
        pieces = []
        for c in range(2 * BOX):
            line = table[j : j + 1, c * LANES : (c + 1) * LANES]
            pieces.append(jnp.where(own_group, jnp.broadcast_to(line, (8, LANES)), 0.0))
        boxes[j] = dot_exact(jnp.concatenate(pieces, axis=0), fold).reshape(BOX, BOX, LANES)

    def split_first(x, _):
        for f in range(FIELDS):
            high, low = halves(term[0, f, x + 2])
            split_term[f, x, :, :LANES] = high
            split_term[f, x, :, LANES:] = low
        return 0

    lax.fori_loop(0, CELL, split_first, 0, unroll=UNROLL)
    load_potential.wait()

    upper = lane >= 64
    row = row_index((CELL, LANES))
    above = jnp.broadcast_to(upper, (CELL, LANES))
    zero = jnp.zeros((CELL, LANES), f32)
    arrivals = info_copies()
    from_xy, from_x, from_y = (info_in.at[i] for i in range(3))
    for h in range(2):
        for i in (1,) if h == 0 else (2, 0):
            arrivals[i].wait_recv()
        low, high = (info, from_x) if h == 0 else (from_y, from_xy)
        atoms = jnp.where(upper, high[...], low[...])

        depth = (atoms[2:3].astype(jnp.int32) + lane % 16) % LANES
        hit = row_index((LANES, LANES)) == depth
        pick = jnp.where(hit, 1.0, 0.0)
        across = pick.T.astype(bf16)
        pick = pick.astype(bf16)
        pick_in[:LANES, h * LANES : (h + 1) * LANES] = pick
        pick_in[LANES:, h * LANES : (h + 1) * LANES] = pick
        pick_out[h * LANES : (h + 1) * LANES] = across
        pick_out[(h + 2) * LANES : (h + 3) * LANES] = across
        for i in range(NPROJ):
            rows = atoms[8 + 4 * i : 12 + 4 * i]
            coupled[i, :, h * LANES : (h + 1) * LANES] = jnp.concatenate([rows] * PAIR, axis=0)

        at_y = atoms[1:2].astype(jnp.int32)
        shift = jnp.broadcast_to(at_y if h == 0 else CELL - at_y, (CELL, LANES))
        bits = []
        for b in range(4):
            step = 1 << b
            stays = row >= step if h == 0 else row < CELL - step
            moved = (shift // step) % 2 == 1
            bits.append((step if h == 0 else CELL - step, moved & stays, moved & ~stays))
        whole = shift >= CELL
        for i in range(BOX):
            for j in range(NPROJ):
                v = boxes[j, i]
                for step, keep, drop in bits:
                    rolled = pltpu.roll(v, step, 0)
                    v = jnp.where(keep, rolled, jnp.where(drop, 0.0, v))
                placed_y[h, j, i] = jnp.where(whole, 0.0, v) if h else v

        at_x = jnp.broadcast_to(atoms[0:1].astype(jnp.int32), (CELL, LANES))
        down = [~above & ((at_x // (1 << b)) % 2 == 1) for b in range(4)]
        up = [above & (((CELL - at_x) // (1 << b)) % 2 == 1) for b in range(4)]
        outside = above & (at_x == 0)
        for j in range(NPROJ):
            v = [placed_y[h, j, i] for i in range(BOX)]
            for b in range(4):
                step = 1 << b
                v = [
                    jnp.where(
                        down[b],
                        v[x - step] if x >= step else zero,
                        jnp.where(up[b], v[x + step] if x + step < CELL else zero, v[x]),
                    )
                    for x in range(CELL)
                ]
            for x in range(CELL):
                frames[h, j, x] = jnp.where(outside, 0.0, v[x])

    def send_shares(n, q, g):
        cells = split_term[pl.ds(PAIR * g, PAIR)].reshape(PAIR * CELL * CELL, 2 * LANES)
        slabs[...] = jnp.dot(cells, pick_in[...], preferred_element_type=f32).reshape(slabs.shape)
        sums = []
        for h in range(2):

            def add(x, totals, h=h):
                frame = [frames[h, j, x] for j in range(NPROJ)]
                new = []
                for o in range(PAIR):
                    part = slabs[o, x, :, h * LANES : (h + 1) * LANES]
                    for j in range(NPROJ):
                        product = part * frame[j]
                        new.append(totals[o * NPROJ + j] + product[:8] + product[8:])
                return tuple(new)

            zero = jnp.zeros((8, LANES), f32)
            totals = lax.fori_loop(0, CELL, add, (zero,) * (PAIR * NPROJ), unroll=UNROLL)
            sums.append(jnp.concatenate([jnp.sum(t, axis=0, keepdims=True) for t in totals], axis=0))
        lines = dot_exact(jnp.concatenate(sums, axis=1), compact[...])
        mine = jnp.zeros((NPROJ, LANES), f32)
        lane4 = lane_index((NPROJ, LANES))
        for o in range(PAIR):
            mine = mine + jnp.where(lane4 // 16 == o, lines[4 * o : 4 * o + 4], 0.0)
        shares[q] = mine
        slot = (lane4 // 4) % 4
        valid = lane4 < PAIR * 16
        for k, (dx, dy) in enumerate(NEAR):
            keep = valid
            if dx:
                keep = keep & (slot % 2 == (1 if dx == 1 else 0))
            if dy:
                keep = keep & (slot // 2 == (1 if dy == 1 else 0))
            moved = pltpu.roll(mine, (4 * dx + 8 * dy) % LANES, 1)
            shares_out[n, g, k] = jnp.where(keep, moved, 0.0)
        for copy in share_copies(n, g):
            copy.start()

    for q in range(2):
        send_shares(0, q, q)

    row16 = row_index((CELL, LANES))

    def make_term(n, q, g, store, spans=((0, CELL),), after=None):
        last, other = n - 1, 1 - g
        for copy in side_copies(last, other):
            copy.wait_recv()

        def stencil(x, _):
            v = pot[x]
            for o in range(PAIR):
                f = PAIR * other + o
                u = term[last, f, x + 2]
                edge = side_y[last, f, x]
                near = term[last, f, x + 1] + term[last, f, x + 3]
                far = term[last, f, x] + term[last, f, x + 4]
                near = near + pltpu.roll(jnp.where(row16 == 0, edge, u), CELL - 1, 0)
                near = near + pltpu.roll(jnp.where(row16 == CELL - 1, edge, u), 1, 0)
                far = far + pltpu.roll(jnp.where(row16 < 2, edge, u), CELL - 2, 0)
                far = far + pltpu.roll(jnp.where(row16 >= CELL - 2, edge, u), 2, 0)
                near = near + pltpu.roll(u, 1, 1) + pltpu.roll(u, LANES - 1, 1)
                far = far + pltpu.roll(u, 2, 1) + pltpu.roll(u, LANES - 2, 1)
                local_part[o, x] = (v + 3.75) * u + (-2.0 / 3.0) * near + (1.0 / 24.0) * far
            return 0

        lax.fori_loop(0, CELL, stencil, 0, unroll=UNROLL)

        for copy in share_copies(last, other):
            copy.wait_recv()
        total = shares[q]
        for k in range(len(NEAR)):
            total = total + shares_in[last, other, k]
        rows = PAIR * NPROJ
        field_of_row = row_index((rows, LANES)) // NPROJ
        field_of_lane = lane_index((rows, LANES)) // 16
        lines = [
            jnp.where(
                field_of_row == field_of_lane, jnp.broadcast_to(total[i : i + 1], (rows, LANES)), 0.0
            )
            for i in range(NPROJ)
        ]
        wide = dot_exact(jnp.concatenate(lines, axis=0), expand[...])
        weights = coupled[0] * wide[:rows]
        for i in range(1, NPROJ):
            weights = weights + coupled[i] * wide[i * rows : (i + 1) * rows]
        coef[...] = weights

        factor = TIME_STEP / (jnp.zeros((CELL, LANES), f32) + n) * (1 - 2 * g)

        def spread(x, _):
            for h in range(2):
                lanes = pl.ds(h * LANES, LANES)
                frame = [frames[h, j, x] for j in range(NPROJ)]
                for o in range(PAIR):
                    value = coef[o * NPROJ : o * NPROJ + 1, lanes] * frame[0]
                    for j in range(1, NPROJ):
                        value = value + coef[o * NPROJ + j : o * NPROJ + j + 1, lanes] * frame[j]
                    high, low = halves(value)
                    split_values[o, x, :, h * LANES : (h + 1) * LANES] = high
                    split_values[o, x, :, (h + 2) * LANES : (h + 3) * LANES] = low
            return 0

        def line(x, _):
            for o in range(PAIR):
                store(PAIR * g + o, x, factor * (local_part[o, x] + projected[o, x]))
            return 0

        for first, end in spans:
            count = end - first
            lax.fori_loop(first, end, spread, 0, unroll=count)
            part = split_values[:, first:end].reshape(PAIR * count * CELL, 4 * LANES)
            projected[:, first:end] = jnp.dot(
                part, pick_out[...], preferred_element_type=f32
            ).reshape(PAIR, count, CELL, LANES)
            lax.fori_loop(first, end, line, 0, unroll=count)
            if after is not None:
                after(first, end)

    def step(m, _):
        n, q = m // 2, m % 2
        g = (n + q) % 2

        def store(f, x, value):
            term[n, f, x + 2] = value
            high, low = halves(value)
            split_term[f, x, :, :LANES] = high
            split_term[f, x, :, LANES:] = low

        make_term(n, q, g, store)
        for copy in side_copies(n, g):
            copy.start()
        send_shares(n, q, g)
        return 0

    lax.fori_loop(2, 2 * STEPS, step, 0)

    def store_last(f, x, value):
        total = term[0, f, x + 2] + term[1, f, x + 2]
        propagated_ref[f, x] = total + term[2, f, x + 2] + term[3, f, x + 2] + value

    occupied = [jnp.broadcast_to(occupations_ref[0:1, o : o + 1], (CELL, LANES)) for o in range(PAIR)]
    middle = CELL // 2

    def density_copy(i):
        half = pl.ds(i * middle, middle)
        return pltpu.make_async_remote_copy(
            src_ref=dens.at[half], dst_ref=dens_in.at[half], send_sem=dens_send.at[i],
            recv_sem=dens_recv.at[i], device_id=partner(), device_id_type=MESH,
        )

    def send_density(first, end):
        def density(x, _):
            total = jnp.zeros((CELL, LANES), f32)
            for f in range(FIELDS):
                total = total + occupied[f % PAIR] * (propagated_ref[f, x] * propagated_ref[f, x])
            dens[x] = total
            return 0

        lax.fori_loop(first, end, density, 0, unroll=end - first)
        density_copy(first // middle).start()

    make_term(STEPS, 0, 0, store_last)
    make_term(STEPS, 1, 1, store_last, ((0, middle), (middle, CELL)), send_density)
    for copy in info_copies():
        copy.wait_send()

    def drain(n, _):
        for g in range(2):
            for copy in side_copies(n, g) + share_copies(n, g):
                copy.wait_send()
        return 0

    lax.fori_loop(0, STEPS, drain, 0)
    for i in range(2):
        density_copy(i).wait_recv()
        half = pl.ds(i * middle, middle)
        density_ref[half] = dens[half] + dens_in[half]
    for i in range(2):
        density_copy(i).wait_send()


def hand_over(propagated_ref, density_ref, propagated_out, density_out, sem):
    copies = [
        pltpu.make_async_copy(propagated_ref.at[f], propagated_out.at[f], sem.at[f])
        for f in range(FIELDS)
    ]
    copies.append(pltpu.make_async_copy(density_ref, density_out, sem.at[FIELDS]))
    for copy in copies:
        copy.start()
    for copy in copies:
        copy.wait()


def local(orbitals, potential, corners, counts, coupling, projectors, occupations):
    fields = orbitals.reshape(FIELDS, CELL, CELL, LANES)
    vmem = pl.BlockSpec(memory_space=pltpu.VMEM)
    hbm = pl.BlockSpec(memory_space=pltpu.HBM)
    grid = (CELL, CELL, LANES)
    dma = pltpu.SemaphoreType.DMA
    near = len(NEAR)
    propagated, density = pl.pallas_call(
        kernel,
        out_shape=(
            pltpu.VMEM((FIELDS,) + grid, f32),
            pltpu.VMEM(grid, f32),
        ),
        in_specs=[hbm] * 7,
        out_specs=(vmem, vmem),
        scratch_shapes=[
            pltpu.VMEM((STEPS, FIELDS, CELL + 4, CELL, LANES), f32),
            pltpu.VMEM((STEPS, FIELDS) + grid, f32),
            pltpu.VMEM((PAIR,) + grid, f32),
            pltpu.VMEM(grid, f32),
            pltpu.VMEM((NPROJ, BOX * BOX * BOX), f32),
            pltpu.VMEM((4, 3), jnp.int32),
            pltpu.VMEM((1, 4), jnp.int32),
            pltpu.VMEM((4, NPROJ, NPROJ), f32),
            pltpu.VMEM((1, PAIR), f32),
            pltpu.VMEM((24, LANES), f32),
            pltpu.VMEM((3, 24, LANES), f32),
            pltpu.VMEM((NPROJ,) + grid, f32),
            pltpu.VMEM((2, NPROJ) + grid, f32),
            pltpu.VMEM((2, NPROJ) + grid, f32),
            pltpu.VMEM((2 * LANES, 2 * LANES), bf16),
            pltpu.VMEM((4 * LANES, LANES), bf16),
            pltpu.VMEM((2 * LANES, LANES), bf16),
            pltpu.VMEM((LANES, 2 * LANES), bf16),
            pltpu.VMEM((NPROJ, PAIR * NPROJ, 2 * LANES), f32),
            pltpu.VMEM((PAIR * NPROJ, 2 * LANES), f32),
            pltpu.VMEM((FIELDS, CELL, CELL, 2 * LANES), bf16),
            pltpu.VMEM((PAIR, CELL, CELL, 2 * LANES), f32),
            pltpu.VMEM((PAIR, CELL, CELL, 4 * LANES), bf16),
            pltpu.VMEM((PAIR,) + grid, f32),
            pltpu.VMEM((2, NPROJ, LANES), f32),
            pltpu.VMEM((STEPS, 2, near, NPROJ, LANES), f32),
            pltpu.VMEM((STEPS, 2, near, NPROJ, LANES), f32),
            pltpu.VMEM(grid, f32),
            pltpu.VMEM(grid, f32),
            dma((FIELDS + 6,)),
            dma((3,)),
            dma((3,)),
            dma((STEPS, 2, 4)),
            dma((STEPS, 2, 4)),
            dma((STEPS, 2, near)),
            dma((STEPS, 2, near)),
            dma((2,)),
            dma((2,)),
        ],
        compiler_params=pltpu.CompilerParams(
            collective_id=1, has_side_effects=True, vmem_limit_bytes=VMEM_BYTES
        ),
    )(
        fields, potential, corners, counts[None], coupling, projectors, occupations[None]
    )
    propagated, density = pl.pallas_call(
        hand_over,
        out_shape=(
            jax.ShapeDtypeStruct((FIELDS,) + grid, f32),
            jax.ShapeDtypeStruct(grid, f32),
        ),
        in_specs=[vmem] * 2,
        out_specs=(hbm, hbm),
        scratch_shapes=[dma((FIELDS + 1,))],
        compiler_params=pltpu.CompilerParams(vmem_limit_bytes=2**20),
    )(propagated, density)
    return propagated.reshape(orbitals.shape), density


def solution(mesh):
    placed = (
        P(None, "band", "gx", "gy", None),
        P("gx", "gy", None),
        P(("gx", "gy"), None),
        P(("gx", "gy")),
        P(("gx", "gy"), None, None),
        P(),
        P("band"),
    )
    return jax.shard_map(
        local,
        mesh=mesh,
        in_specs=placed,
        out_specs=(P(None, "band", "gx", "gy", None), P("gx", "gy", None)),
        check_vma=False,
    )
```

```python
import jax
import jax.numpy as jnp
from jax import lax
from jax.experimental import pallas as pl
from jax.experimental.pallas import tpu as pltpu
from jax.sharding import PartitionSpec as P

BOX = 16
NPROJ = 4
CELL = 16
LANES = 128
FIELDS = 4
STEPS = 4
PAIR = 2
UNROLL = 16
VMEM_BYTES = 60 * 2**20
TIME_STEP = 0.12
MESH = pl.DeviceIdType.MESH
f32 = jnp.float32
bf16 = jnp.bfloat16

NEAR = tuple((dx, dy) for dx in (-1, 1, 0) for dy in (-1, 1, 0) if (dx, dy) != (0, 0))
ABOVE = ((1, 1), (1, 0), (0, 1))
SIDES = ((1, 0), (-1, 0), (0, 1), (0, -1))


def peer(step_x, step_y):
    size_x, size_y = lax.axis_size("gx"), lax.axis_size("gy")
    return (
        lax.rem(lax.axis_index("gx") + step_x + size_x, size_x),
        lax.rem(lax.axis_index("gy") + step_y + size_y, size_y),
        lax.axis_index("band"),
    )


def partner():
    return (lax.axis_index("gx"), lax.axis_index("gy"), 1 - lax.axis_index("band"))


def lane_index(shape):
    return lax.broadcasted_iota(jnp.int32, shape, len(shape) - 1)


def row_index(shape):
    return lax.broadcasted_iota(jnp.int32, shape, len(shape) - 2)


def halves(x):
    high = x.astype(bf16)
    low = (x - high.astype(f32)).astype(bf16)
    return high, low


def thirds(x):
    high = x.astype(bf16)
    rest = x - high.astype(f32)
    mid = rest.astype(bf16)
    low = (rest - mid.astype(f32)).astype(bf16)
    return high, mid, low


def dot_exact(x, pick):
    rows = x.shape[0]
    r = jnp.dot(jnp.concatenate(thirds(x), axis=0), pick, preferred_element_type=f32)
    return r[:rows] + r[rows : 2 * rows] + r[2 * rows :]


def kernel(
    fields_ref, potential_ref, corners_hbm, counts_hbm, coupling_hbm, projectors_ref, occupations_hbm,
    propagated_ref, density_ref,
    term, side_y, local_part, pot, table, corners_ref, counts_ref, coupling_ref, occupations_ref, info, info_in, boxes, placed_y, frames,
    pick_in, pick_out, compact, expand, coupled, coef, split_term, slabs, split_values, projected,
    shares, shares_out, shares_in, dens, dens_in,
    load_sem, info_send, info_recv, side_send, side_recv, share_send, share_recv,
    dens_send, dens_recv,
):
    inner = pl.ds(2, CELL)

    barrier = pltpu.get_barrier_semaphore()
    for d in NEAR:
        pl.semaphore_signal(barrier, inc=1, device_id=peer(*d), device_id_type=MESH)
    pl.semaphore_signal(barrier, inc=1, device_id=partner(), device_id_type=MESH)

    load_fields = [
        pltpu.make_async_copy(fields_ref.at[f], term.at[0, f, inner], load_sem.at[f])
        for f in range(FIELDS)
    ]
    load_potential = pltpu.make_async_copy(potential_ref, pot, load_sem.at[FIELDS])
    load_table = pltpu.make_async_copy(projectors_ref, table, load_sem.at[FIELDS + 1])
    load_atoms = [
        pltpu.make_async_copy(src, dst, load_sem.at[FIELDS + 2 + i])
        for i, (src, dst) in enumerate(
            (
                (corners_hbm, corners_ref),
                (counts_hbm, counts_ref),
                (coupling_hbm, coupling_ref),
                (occupations_hbm, occupations_ref),
            )
        )
    ]
    for copy in load_atoms:
        copy.start()
    load_table.start()
    for copy in load_fields:
        copy.start()
    load_potential.start()

    lane = lane_index((1, LANES))
    atom_of_lane = (lane // BOX) % 4

    for copy in load_atoms:
        copy.wait()

    def over_atoms(values):
        values = [jnp.broadcast_to(v, (1, LANES)) for v in values]
        line = jnp.where(atom_of_lane == 0, values[0], values[1])
        line = jnp.where(atom_of_lane == 2, values[2], line)
        return jnp.where(atom_of_lane == 3, values[3], line)

    for axis in range(3):
        line = over_atoms([corners_ref[a : a + 1, axis : axis + 1] for a in range(4)])
        line = line % CELL if axis < 2 else line
        info[axis : axis + 1] = line.astype(f32)
    count = over_atoms([counts_ref[0:1, a : a + 1] for a in range(4)])
    entry = [
        [over_atoms([coupling_ref[a, j : j + 1, i : i + 1] for a in range(4)]) for i in range(NPROJ)]
        for j in range(NPROJ)
    ]
    for i in range(NPROJ):
        for j in range(NPROJ):
            line = jnp.where(count > max(i, j), 0.5 * (entry[j][i] + entry[i][j]), 0.0)
            info[8 + 4 * i + j : 9 + 4 * i + j] = line

    r = row_index((2 * LANES, LANES))
    l = lane_index((2 * LANES, LANES))
    compact[...] = jnp.where((l < PAIR * 16) & (l % 16 == r // 16), 1.0, 0.0).astype(bf16)
    r = row_index((LANES, 2 * LANES))
    l = lane_index((LANES, 2 * LANES))
    expand[...] = jnp.where(r % 16 == l // 16, 1.0, 0.0).astype(bf16)
    fold = jnp.where(
        row_index((LANES, LANES)) % 16 == lane_index((LANES, LANES)) % 16, 1.0, 0.0
    ).astype(bf16)

    def info_copies():
        return [
            pltpu.make_async_remote_copy(
                src_ref=info, dst_ref=info_in.at[i], send_sem=info_send.at[i],
                recv_sem=info_recv.at[i], device_id=peer(*d), device_id_type=MESH,
            )
            for i, d in enumerate(ABOVE)
        ]

    def side_copies(n, g):
        fields = pl.ds(PAIR * g, PAIR)
        copies = []
        for k, d in enumerate(SIDES):
            if k == 0:
                src, dst = term.at[n, fields, pl.ds(CELL, 2)], term.at[n, fields, pl.ds(0, 2)]
            elif k == 1:
                src, dst = term.at[n, fields, pl.ds(2, 2)], term.at[n, fields, pl.ds(CELL + 2, 2)]
            else:
                rows = pl.ds(CELL - 2, 2) if k == 2 else pl.ds(0, 2)
                src, dst = term.at[n, fields, inner, rows], side_y.at[n, fields, :, rows]
            copies.append(
                pltpu.make_async_remote_copy(
                    src_ref=src, dst_ref=dst, send_sem=side_send.at[n, g, k],
                    recv_sem=side_recv.at[n, g, k], device_id=peer(*d), device_id_type=MESH,
                )
            )
        return copies

    def share_copies(n, g):
        return [
            pltpu.make_async_remote_copy(
                src_ref=shares_out.at[n, g, k], dst_ref=shares_in.at[n, g, k],
                send_sem=share_send.at[n, g, k], recv_sem=share_recv.at[n, g, k],
                device_id=peer(*d), device_id_type=MESH,
            )
            for k, d in enumerate(NEAR)
        ]

    pl.semaphore_wait(barrier, len(NEAR) + 1)

    for copy in info_copies():
        copy.start()
    for copy in load_fields:
        copy.wait()
    for g in range(2):
        for copy in side_copies(0, g):
            copy.start()

    load_table.wait()
    own_group = row_index((8, LANES)) == lane_index((8, LANES)) // 16
    for j in range(NPROJ):
        pieces = []
        for c in range(2 * BOX):
            line = table[j : j + 1, c * LANES : (c + 1) * LANES]
            pieces.append(jnp.where(own_group, jnp.broadcast_to(line, (8, LANES)), 0.0))
        boxes[j] = dot_exact(jnp.concatenate(pieces, axis=0), fold).reshape(BOX, BOX, LANES)

    def split_first(x, _):
        for f in range(FIELDS):
            high, low = halves(term[0, f, x + 2])
            split_term[f, x, :, :LANES] = high
            split_term[f, x, :, LANES:] = low
        return 0

    lax.fori_loop(0, CELL, split_first, 0, unroll=UNROLL)
    load_potential.wait()

    def half_sum(h, at):
        def add(x, totals):
            frame = [frames[h, j, x] for j in range(NPROJ)]
            new = []
            for o in range(PAIR):
                part = slabs[o, x, :, at * LANES : (at + 1) * LANES]
                for j in range(NPROJ):
                    product = part * frame[j]
                    new.append(totals[o * NPROJ + j] + product[:8] + product[8:])
            return tuple(new)

        nothing = jnp.zeros((8, LANES), f32)
        totals = lax.fori_loop(0, CELL, add, (nothing,) * (PAIR * NPROJ), unroll=UNROLL)
        return jnp.concatenate(totals, axis=0)

    first_sums = [[], []]
    upper = lane >= 64
    row = row_index((CELL, LANES))
    above = jnp.broadcast_to(upper, (CELL, LANES))
    zero = jnp.zeros((CELL, LANES), f32)
    arrivals = info_copies()
    from_xy, from_x, from_y = (info_in.at[i] for i in range(3))
    for h in range(2):
        for i in (1,) if h == 0 else (2, 0):
            arrivals[i].wait_recv()
        low, high = (info, from_x) if h == 0 else (from_y, from_xy)
        atoms = jnp.where(upper, high[...], low[...])

        depth = (atoms[2:3].astype(jnp.int32) + lane % 16) % LANES
        hit = row_index((LANES, LANES)) == depth
        pick = jnp.where(hit, 1.0, 0.0)
        across = pick.T.astype(bf16)
        pick = pick.astype(bf16)
        pick_in[:LANES, h * LANES : (h + 1) * LANES] = pick
        pick_in[LANES:, h * LANES : (h + 1) * LANES] = pick
        pick_out[h * LANES : (h + 1) * LANES] = across
        pick_out[(h + 2) * LANES : (h + 3) * LANES] = across
        for i in range(NPROJ):
            rows = atoms[8 + 4 * i : 12 + 4 * i]
            coupled[i, :, h * LANES : (h + 1) * LANES] = jnp.concatenate([rows] * PAIR, axis=0)

        at_y = atoms[1:2].astype(jnp.int32)
        shift = jnp.broadcast_to(at_y if h == 0 else CELL - at_y, (CELL, LANES))
        bits = []
        for b in range(4):
            step = 1 << b
            stays = row >= step if h == 0 else row < CELL - step
            moved = (shift // step) % 2 == 1
            bits.append((step if h == 0 else CELL - step, moved & stays, moved & ~stays))
        whole = shift >= CELL
        for i in range(BOX):
            for j in range(NPROJ):
                v = boxes[j, i]
                for step, keep, drop in bits:
                    rolled = pltpu.roll(v, step, 0)
                    v = jnp.where(keep, rolled, jnp.where(drop, 0.0, v))
                placed_y[h, j, i] = jnp.where(whole, 0.0, v) if h else v

        at_x = jnp.broadcast_to(atoms[0:1].astype(jnp.int32), (CELL, LANES))
        down = [~above & ((at_x // (1 << b)) % 2 == 1) for b in range(4)]
        up = [above & (((CELL - at_x) // (1 << b)) % 2 == 1) for b in range(4)]
        outside = above & (at_x == 0)
        for j in range(NPROJ):
            v = [placed_y[h, j, i] for i in range(BOX)]
            for b in range(4):
                step = 1 << b
                v = [
                    jnp.where(
                        down[b],
                        v[x - step] if x >= step else zero,
                        jnp.where(up[b], v[x + step] if x + step < CELL else zero, v[x]),
                    )
                    for x in range(CELL)
                ]
            for x in range(CELL):
                frames[h, j, x] = jnp.where(outside, 0.0, v[x])

        for g in range(2):
            cells = split_term[pl.ds(PAIR * g, PAIR)].reshape(PAIR * CELL * CELL, 2 * LANES)
            slabs[:, :, :, g * LANES : (g + 1) * LANES] = jnp.dot(
                cells, pick_in[:, h * LANES : (h + 1) * LANES], preferred_element_type=f32
            ).reshape(PAIR, CELL, CELL, LANES)
            first_sums[g].append(half_sum(h, g))

    def inner_products(g):
        cells = split_term[pl.ds(PAIR * g, PAIR)].reshape(PAIR * CELL * CELL, 2 * LANES)
        slabs[...] = jnp.dot(cells, pick_in[...], preferred_element_type=f32).reshape(slabs.shape)
        return [half_sum(h, h) for h in range(2)]

    def send_shares(n, q, g, sums):
        lines = dot_exact(jnp.concatenate(sums, axis=1), compact[...])
        lane4 = lane_index((NPROJ, LANES))
        group = lane_index((8, LANES)) // 16
        mine = []
        for j in range(NPROJ):
            both = jnp.zeros((8, LANES), f32)
            for o in range(PAIR):
                at = 8 * (o * NPROJ + j)
                both = both + jnp.where(group == o, lines[at : at + 8], 0.0)
            mine.append(jnp.sum(both, axis=0, keepdims=True))
        mine = jnp.concatenate(mine, axis=0)
        shares[q] = mine
        slot = (lane4 // 4) % 4
        valid = lane4 < PAIR * 16
        for k, (dx, dy) in enumerate(NEAR):
            keep = valid
            if dx:
                keep = keep & (slot % 2 == (1 if dx == 1 else 0))
            if dy:
                keep = keep & (slot // 2 == (1 if dy == 1 else 0))
            moved = pltpu.roll(mine, (4 * dx + 8 * dy) % LANES, 1)
            shares_out[n, g, k] = jnp.where(keep, moved, 0.0)
        for copy in share_copies(n, g):
            copy.start()

    for q in range(2):
        send_shares(0, q, q, first_sums[q])

    row16 = row_index((CELL, LANES))

    def make_term(n, q, g, store, spans=((0, CELL),), after=None):
        last, other = n - 1, 1 - g
        for copy in side_copies(last, other):
            copy.wait_recv()

        def stencil(x, _):
            v = pot[x]
            for o in range(PAIR):
                f = PAIR * other + o
                u = term[last, f, x + 2]
                edge = side_y[last, f, x]
                near = term[last, f, x + 1] + term[last, f, x + 3]
                far = term[last, f, x] + term[last, f, x + 4]
                near = near + pltpu.roll(jnp.where(row16 == 0, edge, u), CELL - 1, 0)
                near = near + pltpu.roll(jnp.where(row16 == CELL - 1, edge, u), 1, 0)
                far = far + pltpu.roll(jnp.where(row16 < 2, edge, u), CELL - 2, 0)
                far = far + pltpu.roll(jnp.where(row16 >= CELL - 2, edge, u), 2, 0)
                near = near + pltpu.roll(u, 1, 1) + pltpu.roll(u, LANES - 1, 1)
                far = far + pltpu.roll(u, 2, 1) + pltpu.roll(u, LANES - 2, 1)
                local_part[o, x] = (v + 3.75) * u + (-2.0 / 3.0) * near + (1.0 / 24.0) * far
            return 0

        lax.fori_loop(0, CELL, stencil, 0, unroll=UNROLL)

        for copy in share_copies(last, other):
            copy.wait_recv()
        total = shares[q]
        for k in range(len(NEAR)):
            total = total + shares_in[last, other, k]
        rows = PAIR * NPROJ
        field_of_row = row_index((rows, LANES)) // NPROJ
        field_of_lane = lane_index((rows, LANES)) // 16
        lines = [
            jnp.where(
                field_of_row == field_of_lane, jnp.broadcast_to(total[i : i + 1], (rows, LANES)), 0.0
            )
            for i in range(NPROJ)
        ]
        wide = dot_exact(jnp.concatenate(lines, axis=0), expand[...])
        weights = coupled[0] * wide[:rows]
        for i in range(1, NPROJ):
            weights = weights + coupled[i] * wide[i * rows : (i + 1) * rows]
        coef[...] = weights

        factor = TIME_STEP / (jnp.zeros((CELL, LANES), f32) + n) * (1 - 2 * g)

        def spread(x, _):
            for h in range(2):
                lanes = pl.ds(h * LANES, LANES)
                frame = [frames[h, j, x] for j in range(NPROJ)]
                for o in range(PAIR):
                    value = coef[o * NPROJ : o * NPROJ + 1, lanes] * frame[0]
                    for j in range(1, NPROJ):
                        value = value + coef[o * NPROJ + j : o * NPROJ + j + 1, lanes] * frame[j]
                    high, low = halves(value)
                    split_values[o, x, :, h * LANES : (h + 1) * LANES] = high
                    split_values[o, x, :, (h + 2) * LANES : (h + 3) * LANES] = low
            return 0

        def line(x, _):
            for o in range(PAIR):
                store(PAIR * g + o, x, factor * (local_part[o, x] + projected[o, x]))
            return 0

        for first, end in spans:
            count = end - first
            lax.fori_loop(first, end, spread, 0, unroll=count)
            part = split_values[:, first:end].reshape(PAIR * count * CELL, 4 * LANES)
            projected[:, first:end] = jnp.dot(
                part, pick_out[...], preferred_element_type=f32
            ).reshape(PAIR, count, CELL, LANES)
            lax.fori_loop(first, end, line, 0, unroll=count)
            if after is not None:
                after(first, end)

    def step(m, _):
        n, q = m // 2, m % 2
        g = (n + q) % 2

        def store(f, x, value):
            term[n, f, x + 2] = value
            high, low = halves(value)
            split_term[f, x, :, :LANES] = high
            split_term[f, x, :, LANES:] = low

        make_term(n, q, g, store)
        for copy in side_copies(n, g):
            copy.start()
        send_shares(n, q, g, inner_products(g))
        return 0

    lax.fori_loop(2, 2 * STEPS, step, 0)

    def store_last(f, x, value):
        total = term[0, f, x + 2] + term[1, f, x + 2]
        propagated_ref[f, x] = total + term[2, f, x + 2] + term[3, f, x + 2] + value

    occupied = [jnp.broadcast_to(occupations_ref[0:1, o : o + 1], (CELL, LANES)) for o in range(PAIR)]
    middle = CELL // 2

    def density_copy(i):
        half = pl.ds(i * middle, middle)
        return pltpu.make_async_remote_copy(
            src_ref=dens.at[half], dst_ref=dens_in.at[half], send_sem=dens_send.at[i],
            recv_sem=dens_recv.at[i], device_id=partner(), device_id_type=MESH,
        )

    def send_density(first, end):
        def density(x, _):
            total = jnp.zeros((CELL, LANES), f32)
            for f in range(FIELDS):
                total = total + occupied[f % PAIR] * (propagated_ref[f, x] * propagated_ref[f, x])
            dens[x] = total
            return 0

        lax.fori_loop(first, end, density, 0, unroll=end - first)
        density_copy(first // middle).start()

    make_term(STEPS, 0, 0, store_last)
    make_term(STEPS, 1, 1, store_last, ((0, middle), (middle, CELL)), send_density)
    for copy in info_copies():
        copy.wait_send()

    def drain(n, _):
        for g in range(2):
            for copy in side_copies(n, g) + share_copies(n, g):
                copy.wait_send()
        return 0

    lax.fori_loop(0, STEPS, drain, 0)
    for i in range(2):
        density_copy(i).wait_recv()
        half = pl.ds(i * middle, middle)
        density_ref[half] = dens[half] + dens_in[half]
    for i in range(2):
        density_copy(i).wait_send()


def hand_over(propagated_ref, density_ref, propagated_out, density_out, sem):
    copies = [
        pltpu.make_async_copy(propagated_ref.at[f], propagated_out.at[f], sem.at[f])
        for f in range(FIELDS)
    ]
    copies.append(pltpu.make_async_copy(density_ref, density_out, sem.at[FIELDS]))
    for copy in copies:
        copy.start()
    for copy in copies:
        copy.wait()


def local(orbitals, potential, corners, counts, coupling, projectors, occupations):
    fields = orbitals.reshape(FIELDS, CELL, CELL, LANES)
    vmem = pl.BlockSpec(memory_space=pltpu.VMEM)
    hbm = pl.BlockSpec(memory_space=pltpu.HBM)
    grid = (CELL, CELL, LANES)
    dma = pltpu.SemaphoreType.DMA
    near = len(NEAR)
    propagated, density = pl.pallas_call(
        kernel,
        out_shape=(
            pltpu.VMEM((FIELDS,) + grid, f32),
            pltpu.VMEM(grid, f32),
        ),
        in_specs=[hbm] * 7,
        out_specs=(vmem, vmem),
        scratch_shapes=[
            pltpu.VMEM((STEPS, FIELDS, CELL + 4, CELL, LANES), f32),
            pltpu.VMEM((STEPS, FIELDS) + grid, f32),
            pltpu.VMEM((PAIR,) + grid, f32),
            pltpu.VMEM(grid, f32),
            pltpu.VMEM((NPROJ, BOX * BOX * BOX), f32),
            pltpu.VMEM((4, 3), jnp.int32),
            pltpu.VMEM((1, 4), jnp.int32),
            pltpu.VMEM((4, NPROJ, NPROJ), f32),
            pltpu.VMEM((1, PAIR), f32),
            pltpu.VMEM((24, LANES), f32),
            pltpu.VMEM((3, 24, LANES), f32),
            pltpu.VMEM((NPROJ,) + grid, f32),
            pltpu.VMEM((2, NPROJ) + grid, f32),
            pltpu.VMEM((2, NPROJ) + grid, f32),
            pltpu.VMEM((2 * LANES, 2 * LANES), bf16),
            pltpu.VMEM((4 * LANES, LANES), bf16),
            pltpu.VMEM((2 * LANES, LANES), bf16),
            pltpu.VMEM((LANES, 2 * LANES), bf16),
            pltpu.VMEM((NPROJ, PAIR * NPROJ, 2 * LANES), f32),
            pltpu.VMEM((PAIR * NPROJ, 2 * LANES), f32),
            pltpu.VMEM((FIELDS, CELL, CELL, 2 * LANES), bf16),
            pltpu.VMEM((PAIR, CELL, CELL, 2 * LANES), f32),
            pltpu.VMEM((PAIR, CELL, CELL, 4 * LANES), bf16),
            pltpu.VMEM((PAIR,) + grid, f32),
            pltpu.VMEM((2, NPROJ, LANES), f32),
            pltpu.VMEM((STEPS, 2, near, NPROJ, LANES), f32),
            pltpu.VMEM((STEPS, 2, near, NPROJ, LANES), f32),
            pltpu.VMEM(grid, f32),
            pltpu.VMEM(grid, f32),
            dma((FIELDS + 6,)),
            dma((3,)),
            dma((3,)),
            dma((STEPS, 2, 4)),
            dma((STEPS, 2, 4)),
            dma((STEPS, 2, near)),
            dma((STEPS, 2, near)),
            dma((2,)),
            dma((2,)),
        ],
        compiler_params=pltpu.CompilerParams(
            collective_id=1, has_side_effects=True, vmem_limit_bytes=VMEM_BYTES
        ),
    )(
        fields, potential, corners, counts[None], coupling, projectors, occupations[None]
    )
    propagated, density = pl.pallas_call(
        hand_over,
        out_shape=(
            jax.ShapeDtypeStruct((FIELDS,) + grid, f32),
            jax.ShapeDtypeStruct(grid, f32),
        ),
        in_specs=[vmem] * 2,
        out_specs=(hbm, hbm),
        scratch_shapes=[dma((FIELDS + 1,))],
        compiler_params=pltpu.CompilerParams(vmem_limit_bytes=2**20),
    )(propagated, density)
    return propagated.reshape(orbitals.shape), density


def solution(mesh):
    placed = (
        P(None, "band", "gx", "gy", None),
        P("gx", "gy", None),
        P(("gx", "gy"), None),
        P(("gx", "gy")),
        P(("gx", "gy"), None, None),
        P(),
        P("band"),
    )
    return jax.shard_map(
        local,
        mesh=mesh,
        in_specs=placed,
        out_specs=(P(None, "band", "gx", "gy", None), P("gx", "gy", None)),
        check_vma=False,
    )
```
